256 devices in a mesh: orient: 8 (over z), slab: 32 (over y, x, core).
Axes of the slice: x: 4, y: 4, z: 8, core: 2. Of those that a mesh axis runs over, the one named last changes fastest.
Arguments:
- polarization: bfloat16 [16, 2, 3, 32, 9216], P('orient', None, None, 'slab'), may hold values from -6 to 6
- occupied: int32 [32, 9216], P('slab'), may hold values from 0 to 1, as said below
- orient_table: int32 [16, 2], replicated, may hold values from 0 to 15
- dir_index: int32 [2048, 2], replicated, may hold values from 0 to 179
Outputs:
- mueller: float32 [4, 2048], P(None, 'slab')
The draws below stay inside these ranges and needn't reach their ends.
Inputs may be any that keep to these rules, and one draw needn't show every extreme that they name: 1 marks an occupied dipole cell.
All inputs are finite; a program needn't handle non-finite values.
Results may differ from the reference program's by a relative error of at most 0.00087.
Values may be sent and summed in bfloat16 or wider, within the bound.
No kernel may reach another device: no remote copies, remote signals or barrier semaphores. Data moves between devices by JAX's collectives and lax.ppermute only.
A program may use at most 64 MiB of HBM per device.

```python
import math
import jax
import jax.numpy as jnp
from jax import lax

GX = 96
GY = 96
DIRS = 2048
ORIENT_GRID = 16
THETA_GRID = 180
GXY = 9216
GZ = 32
ORIENTS = 16


def draw_occupied(key, part):
    first_key = jax.random.fold_in(key, 11)
    second_key = jax.random.fold_in(key, 23)
    radius = jax.random.randint(first_key, (), 3 * GX // 4, GX + 1)
    planes_iota = jnp.arange(GZ, dtype=jnp.int32)[:, None]
    cells_iota = jnp.arange(GX * GY, dtype=jnp.int32)[None, :]
    offset_x = 2 * (cells_iota % GX) + 1 - GX
    offset_y = 2 * (cells_iota // GX) + 1 - GY
    offset_z = (2 * planes_iota + 1 - GZ) * GX // GZ
    inside = offset_x * offset_x + offset_y * offset_y + offset_z * offset_z <= radius * radius
    keeper = jax.random.randint(second_key, (GZ, GX * GY), 0, 8) != 0
    return (inside & keeper).astype(jnp.int32)


def with_ends(array, own_key, least, high):
    longest = array.shape.index(max(array.shape))
    spots = []
    for shift in (0, 1):
        where = [jax.random.randint(jax.random.fold_in(own_key, axis), (), 0, length) for axis, length in enumerate(array.shape)]
        where[longest] = (where[longest] + shift) % array.shape[longest]
        spots.append(tuple(where))
    return array.at[spots[0]].set(least).at[spots[1]].set(high)


def steps_of(rng, dims, pieces, least, top_value):
    def one(axis_at, blocks):
        steps = jax.random.uniform(jax.random.fold_in(jax.random.fold_in(rng, 6), axis_at), (blocks,), jnp.float32, least / len(pieces), top_value / len(pieces))
        return jnp.repeat(jnp.exp(steps), dims[axis_at] // blocks).reshape((-1,) + (1,) * (len(dims) - axis_at - 1))

    level = one(*pieces[0])
    for cut in pieces[1:]:
        level = level * one(*cut)
    return level


def normal_values(rng, extent, scale, limit, cuts=(), held_as=jnp.bfloat16):
    factor_of = steps_of(rng, extent, cuts, -0.22, 0.18) if cuts else 1.0
    values = jax.random.normal(rng, extent, jnp.float32) * scale * factor_of
    return jnp.minimum(jnp.maximum(values, -limit), limit).astype(held_as)


def setup_inputs(seed: int = 0) -> dict:
    streams_of = jax.random.split(jax.random.key(seed), 5)
    polarization = normal_values(streams_of[0], (ORIENTS, 2, 3, GZ, GXY), 1.0, 6.0, ((0, 8), (3, 32)))
    occupied = draw_occupied(jax.random.fold_in(streams_of[4], 71), 0)
    orient_table = with_ends(jax.random.randint(streams_of[2], (ORIENTS, 2), 0, ORIENT_GRID), jax.random.fold_in(streams_of[2], 1), 0, ORIENT_GRID - 1).astype(jnp.int32)
    dir_index = with_ends(jax.random.randint(streams_of[3], (DIRS, 2), 0, THETA_GRID), jax.random.fold_in(streams_of[3], 1), 0, THETA_GRID - 1).astype(jnp.int32)
    return {"polarization": polarization, "occupied": occupied, "orient_table": orient_table, "dir_index": dir_index}


wave_step = 0.4


def direction_angles(dir_index):
    polar_angle = (dir_index[:, 0].astype(jnp.float32) + 0.5) * (math.pi / THETA_GRID)
    azimuth = dir_index[:, 1].astype(jnp.float32) * (2.0 * math.pi / THETA_GRID)
    return polar_angle, azimuth


def unit_vectors(polar_angle, azimuth):
    return (jnp.sin(polar_angle) * jnp.cos(azimuth), jnp.sin(polar_angle) * jnp.sin(azimuth), jnp.cos(polar_angle))


def phase_block(within, plane_index, normals):
    xcoord = (within % GX).astype(jnp.float32)
    ycoord = (within // GX).astype(jnp.float32)
    zcoord = plane_index.astype(jnp.float32)
    angle = wave_step * (xcoord[:, None] * normals[0][None, :] + ycoord[:, None] * normals[1][None, :] + zcoord[:, None] * normals[2][None, :])
    return jnp.concatenate([jnp.cos(angle), -jnp.sin(angle)], axis=1).astype(jnp.bfloat16)


def orient_weights(orient_table):
    turn_angle = orient_table[:, 0].astype(jnp.float32) * (2.0 * math.pi / ORIENT_GRID)
    weight = jnp.sin((orient_table[:, 1].astype(jnp.float32) + 0.5) * (math.pi / ORIENT_GRID))
    return turn_angle, weight


def mueller_sum(amplitude, orient_table, polar_angle, azimuth):
    turn_angle, weight = orient_weights(orient_table)
    relative = azimuth[None, :] - turn_angle[:, None]
    cos_polar = jnp.cos(polar_angle)[None, :]
    sin_polar = jnp.sin(polar_angle)[None, :]
    cos_turn = jnp.cos(relative)
    sin_turn = jnp.sin(relative)
    parallel = (cos_polar * cos_turn, cos_polar * sin_turn, -sin_polar)
    across = (-sin_turn, cos_turn, None)

    def project(polar_index, basis_set):
        summed = amplitude[:, polar_index, 0] * basis_set[0][:, None, :] + amplitude[:, polar_index, 1] * basis_set[1][:, None, :]
        if basis_set[2] is not None:
            summed = summed + amplitude[:, polar_index, 2] * basis_set[2][:, None, :]
        return summed

    def square(values):
        return values[:, 0] * values[:, 0] + values[:, 1] * values[:, 1]

    lower_right = project(1, across)
    upper_left = project(0, parallel)
    upper_right = project(0, across)
    lower_left = project(1, parallel)
    elem_total = 0.5 * (square(lower_right) + square(upper_left) + square(upper_right) + square(lower_left))
    elem_diff = 0.5 * (square(upper_left) - square(lower_right) + square(lower_left) - square(upper_right))
    elem_real = (lower_right[:, 0] * upper_left[:, 0] + lower_right[:, 1] * upper_left[:, 1]
                 + upper_right[:, 0] * lower_left[:, 0] + upper_right[:, 1] * lower_left[:, 1])
    elem_imag = (upper_left[:, 1] * lower_right[:, 0] - upper_left[:, 0] * lower_right[:, 1]
                 + lower_left[:, 1] * upper_right[:, 0] - lower_left[:, 0] * upper_right[:, 1])
    stacked = jnp.stack([elem_total, elem_diff, elem_real, elem_imag])
    return jnp.sum(stacked * weight[None, :, None], axis=1)


def reference(polarization, occupied, orient_table, dir_index):
    polar_angle, azimuth = direction_angles(dir_index)
    normals = unit_vectors(polar_angle, azimuth)
    masked = polarization * occupied.astype(jnp.bfloat16)[None, None, None]
    cells_all = GZ * GXY
    flattened = masked.reshape(ORIENTS * 6, cells_all)
    block_size = math.gcd(cells_all, 4096)

    def accumulate(summed, block_index):
        offset = block_index * block_size
        segment = lax.dynamic_slice_in_dim(flattened, offset, block_size, 1)
        cell_index = offset + jnp.arange(block_size, dtype=jnp.int32)
        phase = phase_block(cell_index % GXY, cell_index // GXY, normals)
        return summed + jnp.dot(segment, phase, preferred_element_type=jnp.float32), None

    initial = jnp.zeros((ORIENTS * 6, 2 * DIRS), jnp.float32)
    amplitude = lax.scan(accumulate, initial, jnp.arange(cells_all // block_size, dtype=jnp.int32))[0]
    amplitude = amplitude.reshape(ORIENTS, 2, 3, 2, DIRS)
    summed = mueller_sum(amplitude, orient_table, polar_angle, azimuth)
    weight_total = jnp.sum(orient_weights(orient_table)[1])
    return summed / (weight_total * float(GZ * GXY))
```

```python
import functools
import math

import jax
import jax.numpy as jnp
import numpy as np
from jax import lax
from jax.experimental import pallas as pl
from jax.experimental.pallas import tpu as pltpu
from jax.sharding import PartitionSpec as P

GX = 96
GXY = 9216
GZ = 32
DIRS = 2048
ORIENTS = 16
ORIENT_GRID = 16
THETA_GRID = 180
LANES = 128
CHUNK = 384
STEPS = GXY // CHUNK
PARTS = CHUNK // LANES
ROWS = CHUNK // GX
TILES = DIRS // LANES

wave_step = 0.4


def fit_even(function, count):
    nodes = np.cos((np.arange(400) + 0.5) * math.pi / 400)
    square = (nodes + 1.0) * (math.pi * math.pi / 2.0)
    series = np.polynomial.chebyshev.Chebyshev.fit(
        square, function(np.sqrt(square)), count - 1, domain=[0.0, math.pi * math.pi]
    )
    return [float(c) for c in series.convert(kind=np.polynomial.Polynomial).coef]


COS_FIT = fit_even(np.cos, 8)
SIN_FIT = fit_even(lambda r: np.sinc(r / math.pi), 8)


def cos_sin(angle):
    turns = jnp.round(angle * (0.5 / math.pi))
    rest = angle - turns * 6.28125
    rest = rest - turns * (2.0 * math.pi - 6.28125)
    square = rest * rest
    cosine = jnp.full_like(square, COS_FIT[-1])
    for c in COS_FIT[-2::-1]:
        cosine = cosine * square + c
    sine = jnp.full_like(square, SIN_FIT[-1])
    for c in SIN_FIT[-2::-1]:
        sine = sine * square + c
    return cosine, sine * rest


def iota_rows(rows):
    return lax.broadcasted_iota(jnp.int32, (rows, LANES), 0)


def amplitude_kernel(place, pol, occ, dirs, orients, out, basis, polf, lhs, wave, table):
    orient_rank = place[0]
    slab_rank = place[1]
    plane = slab_rank.astype(jnp.float32)

    polar = (dirs[pl.ds(0, TILES, stride=2), :].astype(jnp.float32) + 0.5) * (math.pi / THETA_GRID)
    azimuth = dirs[pl.ds(1, TILES, stride=2), :].astype(jnp.float32) * (2.0 * math.pi / THETA_GRID)
    cos_polar, sin_polar = cos_sin(polar)
    cos_azimuth, sin_azimuth = cos_sin(azimuth)
    wave[0] = wave_step * (sin_polar * cos_azimuth)
    wave[1] = wave_step * (sin_polar * sin_azimuth)
    wave[2] = wave_step * cos_polar
    wave[3] = cos_polar
    wave[4] = sin_polar
    wave[5] = azimuth

    polf[...] = pol[...].astype(jnp.float32)
    for part in range(PARTS):
        mask = occ[pl.ds(part, STEPS, stride=PARTS), :].astype(jnp.float32)
        for incident in range(2):
            block = polf[pl.ds(2 * part + incident, 6 * STEPS, stride=2 * PARTS), :]
            block = (block.reshape(6, STEPS, LANES) * mask[None]).reshape(6 * STEPS, LANES)
            block = block.astype(jnp.bfloat16)
            rows = slice(incident * 6 * STEPS, (incident + 1) * 6 * STEPS)
            lhs[rows, part * LANES : (part + 1) * LANES] = block
            lhs[rows, CHUNK + part * LANES : CHUNK + (part + 1) * LANES] = block

    lane = lax.broadcasted_iota(jnp.int32, (1, LANES), 1)
    own = slab_rank // 2
    swap = slab_rank % 2 == 1

    def own_row(k):
        row = wave[k, pl.ds(own, 1), :]
        turned = pltpu.roll(row, LANES // 2, 1)
        return jnp.where((lane < LANES // 2) == swap, turned, row)

    own_cos, own_sin, own_azimuth = own_row(3), own_row(4), own_row(5)
    tilts = jnp.zeros((1, LANES), jnp.float32)
    for o in range(ORIENTS):
        tilts = jnp.where(lane == o, orients[1, o].astype(jnp.float32), tilts)
    weights = jnp.where(lane < ORIENTS, cos_sin((tilts + 0.5) * (math.pi / ORIENT_GRID))[1], 0.0)
    scale = 1.0 / (jnp.sum(weights, axis=1, keepdims=True) * float(GZ * GXY))
    for o in range(2):
        index = 2 * orient_rank + o
        turn = orients[0, index].astype(jnp.float32) * (2.0 * math.pi / ORIENT_GRID)
        weight = jnp.sum(jnp.where(lane == index, weights, 0.0), axis=1, keepdims=True) * scale
        cos_turn, sin_turn = cos_sin(own_azimuth - turn)
        for k, row in enumerate(
            (own_cos * cos_turn, own_cos * sin_turn, -own_sin, -sin_turn, cos_turn)
        ):
            basis[pl.ds(8 * o + k, 1), :] = row
        basis[pl.ds(8 * o + 5, 1), :] = jnp.broadcast_to(weight, (1, LANES))

    step_rows = iota_rows(8).astype(jnp.float32)
    fine_rows = iota_rows(16)
    coarse = jnp.where(fine_rows < 12, 8 * fine_rows, fine_rows - 12).astype(jnp.float32)
    jumps = (iota_rows(STEPS) * ROWS).astype(jnp.float32)
    half = lax.broadcasted_iota(jnp.int32, (12, LANES), 1) < LANES // 2

    def one_tile(tile, carry):
        along_x = wave[0, pl.ds(tile, 1), :]
        along_y = wave[1, pl.ds(tile, 1), :]
        along_z = wave[2, pl.ds(tile, 1), :]
        base_re, base_im = cos_sin(-(step_rows * along_x + plane * along_z))
        rows_re, rows_im = cos_sin(-(coarse * jnp.where(fine_rows < 12, along_x, along_y)))
        jump_re, jump_im = cos_sin(-(jumps * along_y))
        for a in range(0, 12, 2):
            strip = []
            for k in (a, a + 1):
                turn_re, turn_im = rows_re[k : k + 1], rows_im[k : k + 1]
                strip.append(
                    (
                        base_re * turn_re - base_im * turn_im,
                        base_re * turn_im + base_im * turn_re,
                    )
                )
            strip_re = jnp.concatenate([strip[0][0], strip[1][0]], axis=0)
            strip_im = jnp.concatenate([strip[0][1], strip[1][1]], axis=0)
            for y in range(ROWS):
                turn_re, turn_im = rows_re[12 + y : 13 + y], rows_im[12 + y : 13 + y]
                if y:
                    value_re = strip_re * turn_re - strip_im * turn_im
                    value_im = strip_re * turn_im + strip_im * turn_re
                else:
                    value_re, value_im = strip_re, strip_im
                at = y * GX + 8 * a
                for column, value in ((0, value_re), (LANES, value_im)):
                    high = value.astype(jnp.bfloat16)
                    low = (value - high.astype(jnp.float32)).astype(jnp.bfloat16)
                    table[at : at + 16, column : column + LANES] = high
                    table[CHUNK + at : CHUNK + at + 16, column : column + LANES] = low
        product = jnp.dot(lhs[...], table[...], preferred_element_type=jnp.float32)
        cosines = product[:, :LANES].reshape(12, STEPS, LANES)
        sines = product[:, LANES:].reshape(12, STEPS, LANES)
        real = jnp.sum(cosines * jump_re[None] - sines * jump_im[None], axis=1)
        imag = jnp.sum(cosines * jump_im[None] + sines * jump_re[None], axis=1)
        out[2 * tile] = jnp.where(half, real, pltpu.roll(imag, LANES // 2, 1))
        out[2 * tile + 1] = jnp.where(half, pltpu.roll(real, LANES // 2, 1), imag)
        return carry

    lax.fori_loop(0, TILES, one_tile, 0)


def mueller_kernel(parts, basis, out):
    total = parts[0]
    for k in range(1, GZ):
        total = total + parts[k]

    def project(incident, o, first):
        at = incident * 6 + o * 3
        value = total[at : at + 1] * basis[pl.ds(8 * o + first, 1), :]
        value = value + total[at + 1 : at + 2] * basis[pl.ds(8 * o + first + 1, 1), :]
        if first == 0:
            value = value + total[at + 2 : at + 3] * basis[pl.ds(8 * o + 2, 1), :]
        return value

    def both(value):
        return value + pltpu.roll(value, LANES // 2, 1)

    lane = lax.broadcasted_iota(jnp.int32, (1, LANES), 1)
    sign = jnp.where(lane < LANES // 2, -1.0, 1.0)
    result = [0.0] * 4
    for o in range(2):
        weight = basis[pl.ds(8 * o + 5, 1), :]
        s2, s3 = project(0, o, 0), project(0, o, 3)
        s4, s1 = project(1, o, 0), project(1, o, 3)
        elements = (
            0.5 * (s1 * s1 + s2 * s2 + s3 * s3 + s4 * s4),
            0.5 * (s2 * s2 - s1 * s1 + s4 * s4 - s3 * s3),
            s1 * s2 + s3 * s4,
            sign * (s2 * pltpu.roll(s1, LANES // 2, 1) + s4 * pltpu.roll(s3, LANES // 2, 1)),
        )
        for k in range(4):
            result[k] = result[k] + weight * elements[k]
    final = both(jnp.concatenate(result, axis=0))
    for k in range(out.shape[0]):
        out[k] = final[:, : LANES // 2]


def shards(polarization, occupied, orient_table, dir_index):
    vmem = pl.BlockSpec(memory_space=pltpu.VMEM)
    smem = pl.BlockSpec(memory_space=pltpu.SMEM)
    place = jnp.stack([lax.axis_index("orient"), lax.axis_index("slab")]).astype(jnp.int32)
    pol = polarization.transpose(0, 2, 3, 1, 4).reshape(6, 2, GXY // LANES, LANES)
    pol = pol.transpose(0, 2, 1, 3).reshape(12 * GXY // LANES, LANES)
    occ = occupied.reshape(GXY // LANES, LANES)
    dirs = dir_index.T.reshape(2, TILES, LANES).transpose(1, 0, 2).reshape(2 * TILES, LANES)
    amplitude, basis = pl.pallas_call(
        amplitude_kernel,
        out_shape=(
            jax.ShapeDtypeStruct((GZ, 12, LANES), jnp.float32),
            jax.ShapeDtypeStruct((16, LANES), jnp.float32),
        ),
        in_specs=[smem, vmem, vmem, vmem, smem],
        out_specs=(vmem, vmem),
        scratch_shapes=[
            pltpu.VMEM((12 * GXY // LANES, LANES), jnp.float32),
            pltpu.VMEM((12 * STEPS, 2 * CHUNK), jnp.bfloat16),
            pltpu.VMEM((6, TILES, LANES), jnp.float32),
            pltpu.VMEM((2 * CHUNK, 2 * LANES), jnp.bfloat16),
        ],
        compiler_params=pltpu.CompilerParams(vmem_limit_bytes=24 << 20),
        name="amplitude",
    )(place, pol, occ, dirs, orient_table.T)
    parts = lax.all_to_all(amplitude, "slab", 0, 0, tiled=True)
    orient_size = lax.axis_size("orient")
    copies = pl.pallas_call(
        mueller_kernel,
        out_shape=jax.ShapeDtypeStruct((orient_size, 4, LANES // 2), jnp.float32),
        in_specs=[vmem, vmem],
        out_specs=vmem,
        name="mueller",
    )(parts, basis)
    return jnp.sum(lax.all_to_all(copies, "orient", 0, 0, tiled=True), axis=0)


def solution(mesh):
    return jax.shard_map(
        shards,
        mesh=mesh,
        in_specs=(P("orient", None, None, "slab", None), P("slab", None), P(), P()),
        out_specs=P(None, "slab"),
        check_vma=False,
    )
```

```python
import functools
import math

import jax
import jax.numpy as jnp
import numpy as np
from jax import lax
from jax.experimental import pallas as pl
from jax.experimental.pallas import tpu as pltpu
from jax.sharding import PartitionSpec as P

GX = 96
GXY = 9216
GZ = 32
DIRS = 2048
ORIENTS = 16
ORIENT_GRID = 16
THETA_GRID = 180
LANES = 128
CHUNK = 384
STEPS = GXY // CHUNK
PARTS = CHUNK // LANES
ROWS = CHUNK // GX
TILES = DIRS // LANES

wave_step = 0.4


def fit_even(function, count):
    nodes = np.cos((np.arange(400) + 0.5) * math.pi / 400)
    square = (nodes + 1.0) * (math.pi * math.pi / 2.0)
    series = np.polynomial.chebyshev.Chebyshev.fit(
        square, function(np.sqrt(square)), count - 1, domain=[0.0, math.pi * math.pi]
    )
    return [float(c) for c in series.convert(kind=np.polynomial.Polynomial).coef]


COS_FIT = fit_even(np.cos, 8)
SIN_FIT = fit_even(lambda r: np.sinc(r / math.pi), 8)


def cos_sin(angle):
    turns = jnp.round(angle * (0.5 / math.pi))
    rest = angle - turns * 6.28125
    rest = rest - turns * (2.0 * math.pi - 6.28125)
    square = rest * rest
    cosine = jnp.full_like(square, COS_FIT[-1])
    for c in COS_FIT[-2::-1]:
        cosine = cosine * square + c
    sine = jnp.full_like(square, SIN_FIT[-1])
    for c in SIN_FIT[-2::-1]:
        sine = sine * square + c
    return cosine, sine * rest


def iota_rows(rows):
    return lax.broadcasted_iota(jnp.int32, (rows, LANES), 0)


def amplitude_kernel(pol_hbm, occ_hbm, dirs_hbm, orients_hbm, out, basis, pol, occ, dirs, orients, sems, polf, lhs, wave, table):
    copies = [
        pltpu.make_async_copy(source, target, sems.at[k])
        for k, (source, target) in enumerate(
            ((dirs_hbm, dirs), (pol_hbm, pol), (occ_hbm, occ), (orients_hbm, orients))
        )
    ]
    for copy in copies:
        copy.start()
    orient_rank = lax.axis_index("orient")
    slab_rank = lax.axis_index("slab")
    plane = slab_rank.astype(jnp.float32)

    copies[0].wait()
    polar = (dirs[pl.ds(0, TILES, stride=2), :].astype(jnp.float32) + 0.5) * (math.pi / THETA_GRID)
    azimuth = dirs[pl.ds(1, TILES, stride=2), :].astype(jnp.float32) * (2.0 * math.pi / THETA_GRID)
    cos_polar, sin_polar = cos_sin(polar)
    cos_azimuth, sin_azimuth = cos_sin(azimuth)
    wave[0] = wave_step * (sin_polar * cos_azimuth)
    wave[1] = wave_step * (sin_polar * sin_azimuth)
    wave[2] = wave_step * cos_polar
    wave[3] = cos_polar
    wave[4] = sin_polar
    wave[5] = azimuth

    step_rows = iota_rows(8).astype(jnp.float32)
    fine_rows = iota_rows(16)
    coarse = jnp.where(fine_rows < 12, 8 * fine_rows, fine_rows - 12).astype(jnp.float32)
    jumps = (iota_rows(STEPS) * ROWS).astype(jnp.float32)
    half = lax.broadcasted_iota(jnp.int32, (12, LANES), 1) < LANES // 2

    def make_table(tile, slot):
        along_x = wave[0, pl.ds(tile, 1), :]
        along_y = wave[1, pl.ds(tile, 1), :]
        along_z = wave[2, pl.ds(tile, 1), :]
        base_re, base_im = cos_sin(-(step_rows * along_x + plane * along_z))
        rows_re, rows_im = cos_sin(-(coarse * jnp.where(fine_rows < 12, along_x, along_y)))
        for a in range(0, 12, 2):
            strip = []
            for k in (a, a + 1):
                turn_re, turn_im = rows_re[k : k + 1], rows_im[k : k + 1]
                strip.append(
                    (
                        base_re * turn_re - base_im * turn_im,
                        base_re * turn_im + base_im * turn_re,
                    )
                )
            strip_re = jnp.concatenate([strip[0][0], strip[1][0]], axis=0)
            strip_im = jnp.concatenate([strip[0][1], strip[1][1]], axis=0)
            for y in range(ROWS):
                turn_re, turn_im = rows_re[12 + y : 13 + y], rows_im[12 + y : 13 + y]
                if y:
                    value_re = strip_re * turn_re - strip_im * turn_im
                    value_im = strip_re * turn_im + strip_im * turn_re
                else:
                    value_re, value_im = strip_re, strip_im
                at = y * GX + 8 * a
                for column, value in ((0, value_re), (LANES, value_im)):
                    high = value.astype(jnp.bfloat16)
                    low = (value - high.astype(jnp.float32)).astype(jnp.bfloat16)
                    table[slot, at : at + 16, column : column + LANES] = high
                    table[slot, CHUNK + at : CHUNK + at + 16, column : column + LANES] = low

    def finish(tile, slot):
        product = jnp.dot(lhs[...], table[slot], preferred_element_type=jnp.float32)
        jump_re, jump_im = cos_sin(-(jumps * wave[1, pl.ds(tile, 1), :]))
        cosines = product[:, :LANES].reshape(12, STEPS, LANES)
        sines = product[:, LANES:].reshape(12, STEPS, LANES)
        real = jnp.sum(cosines * jump_re[None] - sines * jump_im[None], axis=1)
        imag = jnp.sum(cosines * jump_im[None] + sines * jump_re[None], axis=1)
        out[2 * tile] = jnp.where(half, real, pltpu.roll(imag, LANES // 2, 1))
        out[2 * tile + 1] = jnp.where(half, pltpu.roll(real, LANES // 2, 1), imag)

    make_table(0, 0)

    copies[1].wait()
    copies[2].wait()
    copies[3].wait()
    polf[...] = pol[...].astype(jnp.float32)
    for part in range(PARTS):
        mask = occ[pl.ds(part, STEPS, stride=PARTS), :].astype(jnp.float32)
        loaded = [
            polf[pl.ds(2 * part + incident, 6 * STEPS, stride=2 * PARTS), :].reshape(2, 3, STEPS, LANES)
            for incident in range(2)
        ]
        block = jnp.concatenate(
            [
                loaded[incident][o, c] * mask
                for c in range(3)
                for incident in range(2)
                for o in range(2)
            ],
            axis=0,
        ).astype(jnp.bfloat16)
        lhs[:, part * LANES : (part + 1) * LANES] = block
        lhs[:, CHUNK + part * LANES : CHUNK + (part + 1) * LANES] = block

    lane = lax.broadcasted_iota(jnp.int32, (1, LANES), 1)
    own = slab_rank // 2
    swap = slab_rank % 2 == 1

    def own_row(k):
        row = wave[k, pl.ds(own, 1), :]
        turned = pltpu.roll(row, LANES // 2, 1)
        return jnp.where((lane < LANES // 2) == swap, turned, row)

    own_cos, own_sin, own_azimuth = own_row(3), own_row(4), own_row(5)
    lane16 = lax.broadcasted_iota(jnp.int32, (1, ORIENTS), 1)
    turns = orients[0:1, :].astype(jnp.float32) * (2.0 * math.pi / ORIENT_GRID)
    weights = cos_sin((orients[1:2, :].astype(jnp.float32) + 0.5) * (math.pi / ORIENT_GRID))[1]
    scale = 1.0 / (jnp.sum(weights, axis=1, keepdims=True) * float(GZ * GXY))
    row4 = lax.broadcasted_iota(jnp.int32, (4, LANES), 0)

    def of_orient(values):
        picked = [
            jnp.sum(jnp.where(lane16 == 2 * orient_rank + o, values, 0.0), axis=1, keepdims=True)
            for o in range(2)
        ]
        return jnp.where(row4 % 2 == 0, picked[0], picked[1])

    cos_turn, sin_turn = cos_sin(own_azimuth - of_orient(turns))
    basis[0, 0:4] = own_cos * cos_turn
    basis[1, 0:4] = own_cos * sin_turn
    basis[2, 0:4] = jnp.broadcast_to(-own_sin, (4, LANES))
    basis[3, 0:4] = -sin_turn
    basis[4, 0:4] = cos_turn
    basis[5, 0:4] = of_orient(weights) * scale

    for tile in range(TILES):
        if tile + 1 < TILES:
            make_table(tile + 1, (tile + 1) % 2)
        finish(tile, tile % 2)


def mueller_kernel(parts, basis, out):
    total = parts[0]
    for k in range(1, GZ):
        total = total + parts[k]
    along = [total[4 * c : 4 * c + 4] for c in range(3)]
    parallel = along[0] * basis[0, 0:4] + along[1] * basis[1, 0:4] + along[2] * basis[2, 0:4]
    across = along[0] * basis[3, 0:4] + along[1] * basis[4, 0:4]
    crossed = jnp.concatenate([across[2:4], across[0:2]], axis=0)
    lane = lax.broadcasted_iota(jnp.int32, (4, LANES), 1)
    turned = pltpu.roll(crossed, LANES // 2, 1) * jnp.where(lane < LANES // 2, -1.0, 1.0)
    weight = basis[5, 0:4]
    weighted = weight * parallel
    same = weighted * parallel
    other = weight * across * across
    elements = (0.5 * (same + other), 0.5 * (same - other), weighted * crossed, weighted * turned)
    rows = [jnp.sum(value, axis=0, keepdims=True) for value in elements]
    final = jnp.concatenate(rows + rows, axis=0)
    for k in range(out.shape[0]):
        out[k] = final


def average_kernel(parts, out):
    total = parts[0]
    for k in range(1, parts.shape[0]):
        total = total + parts[k]
    total = total + pltpu.roll(total, LANES // 2, 1)
    out[...] = total[0:4, : LANES // 2]


def shards(polarization, occupied, orient_table, dir_index):
    vmem = pl.BlockSpec(memory_space=pltpu.VMEM)
    hbm = pl.BlockSpec(memory_space=pltpu.HBM)
    pol = polarization.transpose(0, 2, 3, 1, 4).reshape(6, 2, GXY // LANES, LANES)
    pol = pol.transpose(0, 2, 1, 3).reshape(12 * GXY // LANES, LANES)
    occ = occupied.reshape(GXY // LANES, LANES)
    dirs = dir_index.T.reshape(2, TILES, LANES).transpose(1, 0, 2).reshape(2 * TILES, LANES)
    amplitude, basis = pl.pallas_call(
        amplitude_kernel,
        out_shape=(
            jax.ShapeDtypeStruct((GZ, 12, LANES), jnp.float32),
            jax.ShapeDtypeStruct((6, 8, LANES), jnp.float32),
        ),
        in_specs=[hbm, hbm, hbm, hbm],
        out_specs=(vmem, vmem),
        scratch_shapes=[
            pltpu.VMEM(pol.shape, pol.dtype),
            pltpu.VMEM(occ.shape, occ.dtype),
            pltpu.VMEM(dirs.shape, dirs.dtype),
            pltpu.VMEM((2, ORIENTS), orient_table.dtype),
            pltpu.SemaphoreType.DMA((4,)),
            pltpu.VMEM(pol.shape, jnp.float32),
            pltpu.VMEM((12 * STEPS, 2 * CHUNK), jnp.bfloat16),
            pltpu.VMEM((6, TILES, LANES), jnp.float32),
            pltpu.VMEM((2, 2 * CHUNK, 2 * LANES), jnp.bfloat16),
        ],
        compiler_params=pltpu.CompilerParams(vmem_limit_bytes=24 << 20),
        name="amplitude",
    )(*(pltpu.with_memory_space_constraint(x, pltpu.HBM) for x in (pol, occ, dirs, orient_table.T)))
    parts = lax.all_to_all(amplitude, "slab", 0, 0, tiled=True)
    orient_size = lax.axis_size("orient")
    copies = pl.pallas_call(
        mueller_kernel,
        out_shape=jax.ShapeDtypeStruct((orient_size, 8, LANES), jnp.float32),
        in_specs=[vmem, vmem],
        out_specs=vmem,
        name="mueller",
    )(parts, basis)
    return pl.pallas_call(
        average_kernel,
        out_shape=jax.ShapeDtypeStruct((4, LANES // 2), jnp.float32),
        in_specs=[vmem],
        out_specs=vmem,
        name="average",
    )(lax.all_to_all(copies, "orient", 0, 0, tiled=True))


def solution(mesh):
    return jax.shard_map(
        shards,
        mesh=mesh,
        in_specs=(P("orient", None, None, "slab", None), P("slab", None), P(), P()),
        out_specs=P(None, "slab"),
        check_vma=False,
    )
```

```python
import functools
import math

import jax
import jax.numpy as jnp
import numpy as np
from jax import lax
from jax.experimental import pallas as pl
from jax.experimental.pallas import tpu as pltpu
from jax.sharding import PartitionSpec as P

GX = 96
GXY = 9216
GZ = 32
DIRS = 2048
ORIENTS = 16
ORIENT_GRID = 16
THETA_GRID = 180
LANES = 128
CHUNK = 384
STEPS = GXY // CHUNK
PARTS = CHUNK // LANES
ROWS = CHUNK // GX
TILES = DIRS // LANES
HALVES = 2
SLOTS = 2

wave_step = 0.4


def fit_even(function, count):
    nodes = np.cos((np.arange(400) + 0.5) * math.pi / 400)
    square = (nodes + 1.0) * (math.pi * math.pi / 2.0)
    series = np.polynomial.chebyshev.Chebyshev.fit(
        square, function(np.sqrt(square)), count - 1, domain=[0.0, math.pi * math.pi]
    )
    return [float(c) for c in series.convert(kind=np.polynomial.Polynomial).coef]


COS_FIT = fit_even(np.cos, 8)
SIN_FIT = fit_even(lambda r: np.sinc(r / math.pi), 8)


def cos_sin(angle):
    turns = jnp.round(angle * (0.5 / math.pi))
    rest = angle - turns * 6.28125
    rest = rest - turns * (2.0 * math.pi - 6.28125)
    square = rest * rest
    cosine = jnp.full_like(square, COS_FIT[-1])
    for c in COS_FIT[-2::-1]:
        cosine = cosine * square + c
    sine = jnp.full_like(square, SIN_FIT[-1])
    for c in SIN_FIT[-2::-1]:
        sine = sine * square + c
    return cosine, sine * rest


def times(a, b):
    return a[0] * b[0] - a[1] * b[1], a[0] * b[1] + a[1] * b[0]


def rows_of(shape):
    return lax.broadcasted_iota(jnp.int32, shape, 0)


def between(rows, first, count):
    return ((rows - first) & 7) < count


def sum_rows(tiles):
    rows = rows_of((8, LANES))
    by_four = []
    for k, first in ((3, 0), (1, 6), (2, 7), (0, 5)):
        mask = between(rows, first, 4)
        here, there = tiles[k], tiles[k + 4]
        by_four.append(
            jnp.where(mask, here, there) + pltpu.roll(jnp.where(mask, there, here), 4, 0)
        )
    by_two = []
    for k, first in ((0, 2), (2, 1)):
        mask = between(rows, first, 2) | between(rows, first + 4, 2)
        here, there = by_four[k], by_four[k + 1]
        by_two.append(
            jnp.where(mask, here, there) + pltpu.roll(jnp.where(mask, there, here), 2, 0)
        )
    mask = (rows & 1) == 1
    here, there = by_two
    return jnp.where(mask, here, there) + pltpu.roll(jnp.where(mask, there, here), 1, 0)


def amplitude_kernel(
    pol_hbm, occ_hbm, dirs_hbm, orients_hbm, out, pol, occ, dirs, orients, sems, polf, lhs, rows, base, jump, table
):
    copies = [
        pltpu.make_async_copy(source, target, sems.at[k])
        for k, (source, target) in enumerate(
            ((dirs_hbm, dirs), (orients_hbm, orients), (pol_hbm, pol), (occ_hbm, occ))
        )
    ]
    for copy in copies:
        copy.start()
    orient_rank = lax.axis_index("orient")
    slab_rank = lax.axis_index("slab")
    plane = slab_rank.astype(jnp.float32)

    copies[0].wait()
    polar = (dirs[pl.ds(0, TILES, stride=2), :].astype(jnp.float32) + 0.5) * (math.pi / THETA_GRID)
    azimuth = dirs[pl.ds(1, TILES, stride=2), :].astype(jnp.float32) * (2.0 * math.pi / THETA_GRID)
    cos_polar, sin_polar = cos_sin(polar)
    cos_azimuth, sin_azimuth = cos_sin(azimuth)

    x1 = cos_sin(-wave_step * (sin_polar * cos_azimuth))
    y1 = cos_sin(-wave_step * (sin_polar * sin_azimuth))
    z = cos_sin(-wave_step * plane * cos_polar)
    x2 = times(x1, x1)
    x3 = times(x2, x1)
    x4 = times(x2, x2)
    x8 = times(x4, x4)
    fine = [None, x1, x2, x3, x4, times(x4, x1), times(x4, x2), times(x4, x3)]
    for k in range(8):
        value = times(z, fine[k]) if k else z
        for part in range(2):
            base[part, pl.ds(k, TILES, stride=8), :] = value[part]
    coarse = x4
    for k in range(6):
        rows[2 * k], rows[2 * k + 1] = coarse
        coarse = times(coarse, x8)
    rows[12], rows[13] = y1
    y2 = times(y1, y1)
    powers = [(jnp.ones_like(polar), jnp.zeros_like(polar)), times(y2, y2)]
    for k in range(2, STEPS):
        powers.append(times(powers[k // 2], powers[k - k // 2]))
    for k in range(STEPS):
        for part in range(2):
            jump[part, pl.ds(k, TILES, stride=STEPS), :] = powers[k][part]

    copies[1].wait()
    lane16 = lax.broadcasted_iota(jnp.int32, (1, ORIENTS), 1)
    turns = orients[0:1, :].astype(jnp.float32) * (2.0 * math.pi / ORIENT_GRID)
    weights = cos_sin((orients[1:2, :].astype(jnp.float32) + 0.5) * (math.pi / ORIENT_GRID))[1]
    shares = weights / (jnp.sum(weights, axis=1, keepdims=True) * float(GZ * GXY))
    for o in range(2):
        mine = lane16 == 2 * orient_rank + o
        turn = jnp.sum(jnp.where(mine, turns, 0.0), axis=1, keepdims=True)
        root = jnp.sqrt(jnp.sum(jnp.where(mine, shares, 0.0), axis=1, keepdims=True))
        cos_turn, sin_turn = cos_sin(azimuth - turn)
        cos_turn, sin_turn = cos_turn * root, sin_turn * root
        at = 14 + 5 * o
        rows[at] = cos_polar * cos_turn
        rows[at + 1] = cos_polar * sin_turn
        rows[at + 2] = -sin_polar * root
        rows[at + 3] = -sin_turn
        rows[at + 4] = cos_turn

    half = lax.broadcasted_iota(jnp.int32, (8, LANES), 1) < LANES // 2

    def make_table(tile, slot):
        start_re, start_im = base[0, 8 * tile : 8 * tile + 8, :], base[1, 8 * tile : 8 * tile + 8, :]
        y_re, y_im = rows[12, tile : tile + 1, :], rows[13, tile : tile + 1, :]
        strips = [None] * 12
        for k in range(6):
            turn_re, turn_im = rows[2 * k, tile : tile + 1, :], rows[2 * k + 1, tile : tile + 1, :]
            rr, ii, ri, ir = start_re * turn_re, start_im * turn_im, start_re * turn_im, start_im * turn_re
            strips[6 + k] = (rr - ii, ri + ir)
            strips[5 - k] = (rr + ii, ir - ri)
        twice = y_re + y_re
        for a in range(0, 12, 2):
            line = [[None, None] for _ in range(ROWS)]
            for k in range(2):
                v_re, v_im = strips[a + k]
                rr, ii, ri, ir = v_re * y_re, v_im * y_im, v_re * y_im, v_im * y_re
                after = (rr - ii, ri + ir)
                line[0][k] = (rr + ii, ir - ri)
                line[1][k] = (v_re, v_im)
                line[2][k] = after
                line[3][k] = (twice * after[0] - v_re, twice * after[1] - v_im)
            for y in range(ROWS):
                at = y * GX + 8 * a
                for part in range(2):
                    value = jnp.concatenate([line[y][0][part], line[y][1][part]], axis=0)
                    columns = slice(part * LANES, (part + 1) * LANES)
                    high = value.astype(jnp.bfloat16)
                    table[slot, at : at + 16, columns] = high
                    if HALVES == 2:
                        low = (value - high.astype(jnp.float32)).astype(jnp.bfloat16)
                        table[slot, CHUNK + at : CHUNK + at + 16, columns] = low

    def finish(tile, slot):
        product = jnp.dot(lhs[...], table[slot], preferred_element_type=jnp.float32)
        jump_re = jump[0, STEPS * tile : STEPS * tile + STEPS, :].reshape(3, 8, LANES)
        jump_im = jump[1, STEPS * tile : STEPS * tile + STEPS, :].reshape(3, 8, LANES)
        sums = []
        for group in range(12):
            at = STEPS * group
            c = [product[at + 8 * h : at + 8 * h + 8, :LANES] for h in range(3)]
            s = [product[at + 8 * h : at + 8 * h + 8, LANES:] for h in range(3)]
            real = sum(c[h] * jump_re[h] for h in range(3)) - sum(s[h] * jump_im[h] for h in range(3))
            imag = sum(c[h] * jump_im[h] + s[h] * jump_re[h] for h in range(3))
            sums.append((real, imag))
        row = [rows[14 + k, tile : tile + 1, :] for k in range(10)]
        result = []
        for part in range(2):
            tiles = []
            for incident in range(2):
                for o in range(2):
                    along = [sums[4 * c + 2 * incident + o][part] for c in range(3)]
                    tiles.append(sum(along[c] * row[5 * o + c] for c in range(3)))
            for incident in (1, 0):
                for o in range(2):
                    along = [sums[4 * c + 2 * incident + o][part] for c in range(2)]
                    tiles.append(sum(along[c] * row[5 * o + 3 + c] for c in range(2)))
            result.append(sum_rows(tiles))
        real, imag = result
        out[2 * tile] = jnp.where(half, real, pltpu.roll(imag, LANES // 2, 1))
        out[2 * tile + 1] = jnp.where(half, pltpu.roll(real, LANES // 2, 1), imag)

    make_table(0, 0)

    copies[2].wait()
    copies[3].wait()
    polf[...] = pol[...].astype(jnp.float32)
    for part in range(PARTS):
        mask = occ[pl.ds(part, STEPS, stride=PARTS), :].astype(jnp.float32)
        loaded = [
            polf[pl.ds(2 * part + incident, 6 * STEPS, stride=2 * PARTS), :].reshape(2, 3, STEPS, LANES)
            for incident in range(2)
        ]
        block = jnp.concatenate(
            [
                loaded[incident][o, c] * mask
                for c in range(3)
                for incident in range(2)
                for o in range(2)
            ],
            axis=0,
        ).astype(jnp.bfloat16)
        for copy in range(HALVES):
            at = copy * CHUNK + part * LANES
            lhs[:, at : at + LANES] = block

    for tile in range(TILES):
        if tile + 1 < TILES:
            make_table(tile + 1, (tile + 1) % SLOTS)
        finish(tile, tile % SLOTS)


def mueller_kernel(parts, out):
    total = parts[0]
    for k in range(1, GZ):
        total = total + parts[k]
    other = pltpu.roll(total, 4, 0)
    lane = lax.broadcasted_iota(jnp.int32, (8, LANES), 1)
    side = jnp.where(rows_of((8, LANES)) < 4, 0.5, -0.5)
    turned = pltpu.roll(other, LANES // 2, 1) * jnp.where(lane < LANES // 2, -side, side)
    square = total * total
    elements = [0.5 * square, side * square, 0.5 * (total * other), total * turned]
    final = sum_rows(elements + elements)
    for k in range(out.shape[0]):
        out[k] = final


def average_kernel(parts, out):
    total = parts[0]
    for k in range(1, parts.shape[0]):
        total = total + parts[k]
    total = total + pltpu.roll(total, LANES // 2, 1)
    out[...] = total[0:4, : LANES // 2]


VMEM = pl.BlockSpec(memory_space=pltpu.VMEM)
HBM = pl.BlockSpec(memory_space=pltpu.HBM)


def amplitudes(polarization, occupied, orient_table, dir_index):
    pol = polarization.transpose(0, 2, 3, 1, 4).reshape(6, 2, GXY // LANES, LANES)
    pol = pol.transpose(0, 2, 1, 3).reshape(12 * GXY // LANES, LANES)
    occ = occupied.reshape(GXY // LANES, LANES)
    dirs = dir_index.T.reshape(2, TILES, LANES).transpose(1, 0, 2).reshape(2 * TILES, LANES)
    operands = (pol, occ, dirs, orient_table.T)
    return pl.pallas_call(
        amplitude_kernel,
        out_shape=pltpu.VMEM((GZ, 8, LANES), jnp.float32),
        in_specs=[HBM] * 4,
        out_specs=VMEM,
        scratch_shapes=[pltpu.VMEM(x.shape, x.dtype) for x in operands]
        + [
            pltpu.SemaphoreType.DMA((4,)),
            pltpu.VMEM(pol.shape, jnp.float32),
            pltpu.VMEM((12 * STEPS, HALVES * CHUNK), jnp.bfloat16),
            pltpu.VMEM((24, TILES, LANES), jnp.float32),
            pltpu.VMEM((2, 8 * TILES, LANES), jnp.float32),
            pltpu.VMEM((2, STEPS * TILES, LANES), jnp.float32),
            pltpu.VMEM((SLOTS, HALVES * CHUNK, 2 * LANES), jnp.bfloat16),
        ],
        compiler_params=pltpu.CompilerParams(vmem_limit_bytes=24 << 20),
        name="amplitude",
    )(*(pltpu.with_memory_space_constraint(x, pltpu.HBM) for x in operands))


def shards(polarization, occupied, orient_table, dir_index):
    amplitude = amplitudes(polarization, occupied, orient_table, dir_index)
    parts = lax.all_to_all(amplitude, "slab", 0, 0, tiled=True)
    copies = pl.pallas_call(
        mueller_kernel,
        out_shape=pltpu.VMEM((lax.axis_size("orient"), 8, LANES), jnp.float32),
        in_specs=[VMEM],
        out_specs=VMEM,
        name="mueller",
    )(pltpu.with_memory_space_constraint(parts, pltpu.VMEM))
    parts = lax.all_to_all(copies, "orient", 0, 0, tiled=True)
    return pl.pallas_call(
        average_kernel,
        out_shape=jax.ShapeDtypeStruct((4, LANES // 2), jnp.float32),
        in_specs=[VMEM],
        out_specs=VMEM,
        name="average",
    )(pltpu.with_memory_space_constraint(parts, pltpu.VMEM))


def solution(mesh):
    return jax.shard_map(
        shards,
        mesh=mesh,
        in_specs=(P("orient", None, None, "slab", None), P("slab", None), P(), P()),
        out_specs=P(None, "slab"),
        check_vma=False,
    )
```

```python
import functools
import math

import jax
import jax.numpy as jnp
import numpy as np
from jax import lax
from jax.experimental import pallas as pl
from jax.experimental.pallas import tpu as pltpu
from jax.sharding import PartitionSpec as P

GX = 96
GXY = 9216
GZ = 32
DIRS = 2048
ORIENTS = 16
ORIENT_GRID = 16
THETA_GRID = 180
LANES = 128
CHUNK = 384
STEPS = GXY // CHUNK
PARTS = CHUNK // LANES
ROWS = CHUNK // GX
TILES = DIRS // LANES

wave_step = 0.4


def fit_even(function, count):
    nodes = np.cos((np.arange(400) + 0.5) * math.pi / 400)
    square = (nodes + 1.0) * (math.pi * math.pi / 2.0)
    series = np.polynomial.chebyshev.Chebyshev.fit(
        square, function(np.sqrt(square)), count - 1, domain=[0.0, math.pi * math.pi]
    )
    return [float(c) for c in series.convert(kind=np.polynomial.Polynomial).coef]


COS_FIT = fit_even(np.cos, 8)
SIN_FIT = fit_even(lambda r: np.sinc(r / math.pi), 8)


def cos_sin(angle):
    turns = jnp.round(angle * (0.5 / math.pi))
    rest = angle - turns * 6.28125
    rest = rest - turns * (2.0 * math.pi - 6.28125)
    square = rest * rest
    cosine = jnp.full_like(square, COS_FIT[-1])
    for c in COS_FIT[-2::-1]:
        cosine = cosine * square + c
    sine = jnp.full_like(square, SIN_FIT[-1])
    for c in SIN_FIT[-2::-1]:
        sine = sine * square + c
    return cosine, sine * rest


def times(a, b):
    return a[0] * b[0] - a[1] * b[1], a[0] * b[1] + a[1] * b[0]


def rows_of(shape):
    return lax.broadcasted_iota(jnp.int32, shape, 0)


def between(rows, first, count):
    return ((rows - first) & 7) < count


def sum_rows(tiles):
    rows = rows_of((8, LANES))
    by_four = []
    for k, first in ((3, 0), (1, 6), (2, 7), (0, 5)):
        mask = between(rows, first, 4)
        here, there = tiles[k], tiles[k + 4]
        by_four.append(
            jnp.where(mask, here, there) + pltpu.roll(jnp.where(mask, there, here), 4, 0)
        )
    by_two = []
    for k, first in ((0, 2), (2, 1)):
        mask = between(rows, first, 2) | between(rows, first + 4, 2)
        here, there = by_four[k], by_four[k + 1]
        by_two.append(
            jnp.where(mask, here, there) + pltpu.roll(jnp.where(mask, there, here), 2, 0)
        )
    mask = (rows & 1) == 1
    here, there = by_two
    return jnp.where(mask, here, there) + pltpu.roll(jnp.where(mask, there, here), 1, 0)


def amplitude_kernel(
    pol_hbm, occ_hbm, dirs_hbm, orients_hbm, out, pol, occ, dirs, orients, sems, polf, lhs, rows, base, jump, table
):
    copies = [
        pltpu.make_async_copy(source, target, sems.at[k])
        for k, (source, target) in enumerate(
            ((dirs_hbm, dirs), (orients_hbm, orients), (pol_hbm, pol), (occ_hbm, occ))
        )
    ]
    for copy in copies:
        copy.start()
    orient_rank = lax.axis_index("orient")
    slab_rank = lax.axis_index("slab")
    plane = slab_rank.astype(jnp.float32)

    copies[0].wait()
    polar = (dirs[pl.ds(0, TILES, stride=2), :].astype(jnp.float32) + 0.5) * (math.pi / THETA_GRID)
    azimuth = dirs[pl.ds(1, TILES, stride=2), :].astype(jnp.float32) * (2.0 * math.pi / THETA_GRID)
    cos_polar, sin_polar = cos_sin(polar)
    cos_azimuth, sin_azimuth = cos_sin(azimuth)

    x1 = cos_sin(-wave_step * (sin_polar * cos_azimuth))
    y1 = cos_sin(-wave_step * (sin_polar * sin_azimuth))
    z = cos_sin(-wave_step * plane * cos_polar)
    x2 = times(x1, x1)
    x3 = times(x2, x1)
    x4 = times(x2, x2)
    x8 = times(x4, x4)
    fine = [None, x1, x2, x3, x4, times(x4, x1), times(x4, x2), times(x4, x3)]
    for k in range(8):
        value = times(z, fine[k]) if k else z
        for part in range(2):
            base[part, pl.ds(k, TILES, stride=8), :] = value[part]
    coarse = x4
    for k in range(6):
        rows[2 * k], rows[2 * k + 1] = coarse
        coarse = times(coarse, x8)
    rows[12], rows[13] = y1
    y2 = times(y1, y1)
    powers = [(jnp.ones_like(polar), jnp.zeros_like(polar)), times(y2, y2)]
    for k in range(2, STEPS):
        powers.append(times(powers[k // 2], powers[k - k // 2]))
    for k in range(STEPS):
        for part in range(2):
            jump[part, pl.ds(k, TILES, stride=STEPS), :] = powers[k][part]

    copies[1].wait()
    lane16 = lax.broadcasted_iota(jnp.int32, (1, ORIENTS), 1)
    turns = orients[0:1, :].astype(jnp.float32) * (2.0 * math.pi / ORIENT_GRID)
    weights = cos_sin((orients[1:2, :].astype(jnp.float32) + 0.5) * (math.pi / ORIENT_GRID))[1]
    shares = weights / (jnp.sum(weights, axis=1, keepdims=True) * float(GZ * GXY))
    for o in range(2):
        mine = lane16 == 2 * orient_rank + o
        turn = jnp.sum(jnp.where(mine, turns, 0.0), axis=1, keepdims=True)
        root = jnp.sqrt(jnp.sum(jnp.where(mine, shares, 0.0), axis=1, keepdims=True))
        cos_turn, sin_turn = cos_sin(azimuth - turn)
        cos_turn, sin_turn = cos_turn * root, sin_turn * root
        at = 14 + 5 * o
        rows[at] = cos_polar * cos_turn
        rows[at + 1] = cos_polar * sin_turn
        rows[at + 2] = -sin_polar * root
        rows[at + 3] = -sin_turn
        rows[at + 4] = cos_turn

    half = lax.broadcasted_iota(jnp.int32, (8, LANES), 1) < LANES // 2

    def make_table(tile, slot):
        start_re, start_im = base[0, 8 * tile : 8 * tile + 8, :], base[1, 8 * tile : 8 * tile + 8, :]
        y_re, y_im = rows[12, tile : tile + 1, :], rows[13, tile : tile + 1, :]
        strips = [None] * 12
        for k in range(6):
            turn_re, turn_im = rows[2 * k, tile : tile + 1, :], rows[2 * k + 1, tile : tile + 1, :]
            rr, ii, ri, ir = start_re * turn_re, start_im * turn_im, start_re * turn_im, start_im * turn_re
            strips[6 + k] = (rr - ii, ri + ir)
            strips[5 - k] = (rr + ii, ir - ri)
        twice = y_re + y_re
        for a in range(0, 12, 2):
            line = [[None, None] for _ in range(ROWS)]
            for k in range(2):
                v_re, v_im = strips[a + k]
                rr, ii, ri, ir = v_re * y_re, v_im * y_im, v_re * y_im, v_im * y_re
                after = (rr - ii, ri + ir)
                line[0][k] = (rr + ii, ir - ri)
                line[1][k] = (v_re, v_im)
                line[2][k] = after
                line[3][k] = (twice * after[0] - v_re, twice * after[1] - v_im)
            for y in range(ROWS):
                at = y * GX + 8 * a
                for part in range(2):
                    value = jnp.concatenate([line[y][0][part], line[y][1][part]], axis=0)
                    columns = slice(part * LANES, (part + 1) * LANES)
                    table[slot, at : at + 16, columns] = value.astype(jnp.bfloat16)

    def finish(tile, slot):
        product = jnp.dot(lhs[...], table[slot], preferred_element_type=jnp.float32)
        jump_re = jump[0, STEPS * tile : STEPS * tile + STEPS, :].reshape(3, 8, LANES)
        jump_im = jump[1, STEPS * tile : STEPS * tile + STEPS, :].reshape(3, 8, LANES)
        sums = []
        for group in range(12):
            at = STEPS * group
            c = [product[at + 8 * h : at + 8 * h + 8, :LANES] for h in range(3)]
            s = [product[at + 8 * h : at + 8 * h + 8, LANES:] for h in range(3)]
            real = sum(c[h] * jump_re[h] for h in range(3)) - sum(s[h] * jump_im[h] for h in range(3))
            imag = sum(c[h] * jump_im[h] + s[h] * jump_re[h] for h in range(3))
            sums.append((real, imag))
        row = [rows[14 + k, tile : tile + 1, :] for k in range(10)]
        result = []
        for part in range(2):
            tiles = []
            for incident in range(2):
                for o in range(2):
                    along = [sums[4 * c + 2 * incident + o][part] for c in range(3)]
                    tiles.append(sum(along[c] * row[5 * o + c] for c in range(3)))
            for incident in (1, 0):
                for o in range(2):
                    along = [sums[4 * c + 2 * incident + o][part] for c in range(2)]
                    tiles.append(sum(along[c] * row[5 * o + 3 + c] for c in range(2)))
            result.append(sum_rows(tiles))
        real, imag = result
        out[2 * tile] = jnp.where(half, real, pltpu.roll(imag, LANES // 2, 1))
        out[2 * tile + 1] = jnp.where(half, pltpu.roll(real, LANES // 2, 1), imag)

    make_table(0, 0)

    for copy in copies[2:]:
        copy.wait()
    polf[...] = pol[...].astype(jnp.float32)
    for part in range(PARTS):
        mask = occ[pl.ds(part, STEPS, stride=PARTS), :].astype(jnp.float32)
        loaded = [
            polf[pl.ds(2 * part + incident, 6 * STEPS, stride=2 * PARTS), :].reshape(2, 3, STEPS, LANES)
            for incident in range(2)
        ]
        lhs[:, part * LANES : (part + 1) * LANES] = jnp.concatenate(
            [
                loaded[incident][o, c] * mask
                for c in range(3)
                for incident in range(2)
                for o in range(2)
            ],
            axis=0,
        ).astype(jnp.bfloat16)

    for tile in range(TILES):
        if tile + 1 < TILES:
            make_table(tile + 1, (tile + 1) % 2)
        finish(tile, tile % 2)


def mueller_kernel(parts, out):
    total = parts[0]
    for k in range(1, GZ):
        total = total + parts[k]
    other = pltpu.roll(total, 4, 0)
    lane = lax.broadcasted_iota(jnp.int32, (8, LANES), 1)
    side = jnp.where(rows_of((8, LANES)) < 4, 0.5, -0.5)
    turned = pltpu.roll(other, LANES // 2, 1) * jnp.where(lane < LANES // 2, -side, side)
    square = total * total
    elements = [0.5 * square, side * square, 0.5 * (total * other), total * turned]
    final = sum_rows(elements + elements)
    for k in range(out.shape[0]):
        out[k] = final


def average_kernel(parts, out):
    total = parts[0]
    for k in range(1, parts.shape[0]):
        total = total + parts[k]
    total = total + pltpu.roll(total, LANES // 2, 1)
    out[...] = total[0:4, : LANES // 2]


VMEM = pl.BlockSpec(memory_space=pltpu.VMEM)
HBM = pl.BlockSpec(memory_space=pltpu.HBM)


def amplitudes(polarization, occupied, orient_table, dir_index):
    pol = polarization.transpose(0, 2, 3, 1, 4).reshape(6, 2, GXY // LANES, LANES)
    pol = pol.transpose(0, 2, 1, 3).reshape(12 * GXY // LANES, LANES)
    occ = occupied.reshape(GXY // LANES, LANES)
    dirs = dir_index.T.reshape(2, TILES, LANES).transpose(1, 0, 2).reshape(2 * TILES, LANES)
    operands = (pol, occ, dirs, orient_table.T)
    return pl.pallas_call(
        amplitude_kernel,
        out_shape=pltpu.VMEM((GZ, 8, LANES), jnp.float32),
        in_specs=[HBM] * 4,
        out_specs=VMEM,
        scratch_shapes=[pltpu.VMEM(x.shape, x.dtype) for x in operands]
        + [
            pltpu.SemaphoreType.DMA((4,)),
            pltpu.VMEM(pol.shape, jnp.float32),
            pltpu.VMEM((12 * STEPS, CHUNK), jnp.bfloat16),
            pltpu.VMEM((24, TILES, LANES), jnp.float32),
            pltpu.VMEM((2, 8 * TILES, LANES), jnp.float32),
            pltpu.VMEM((2, STEPS * TILES, LANES), jnp.float32),
            pltpu.VMEM((2, CHUNK, 2 * LANES), jnp.bfloat16),
        ],
        compiler_params=pltpu.CompilerParams(vmem_limit_bytes=24 << 20),
        name="amplitude",
    )(*(pltpu.with_memory_space_constraint(x, pltpu.HBM) for x in operands))


def shards(polarization, occupied, orient_table, dir_index):
    amplitude = amplitudes(polarization, occupied, orient_table, dir_index)
    parts = lax.all_to_all(amplitude, "slab", 0, 0, tiled=True)
    copies = pl.pallas_call(
        mueller_kernel,
        out_shape=pltpu.VMEM((lax.axis_size("orient"), 8, LANES), jnp.float32),
        in_specs=[VMEM],
        out_specs=VMEM,
        name="mueller",
    )(pltpu.with_memory_space_constraint(parts, pltpu.VMEM))
    parts = lax.all_to_all(copies, "orient", 0, 0, tiled=True)
    return pl.pallas_call(
        average_kernel,
        out_shape=jax.ShapeDtypeStruct((4, LANES // 2), jnp.float32),
        in_specs=[VMEM],
        out_specs=VMEM,
        name="average",
    )(pltpu.with_memory_space_constraint(parts, pltpu.VMEM))


def solution(mesh):
    return jax.shard_map(
        shards,
        mesh=mesh,
        in_specs=(P("orient", None, None, "slab", None), P("slab", None), P(), P()),
        out_specs=P(None, "slab"),
        check_vma=False,
    )
```

```python
import functools
import math

import jax
import jax.numpy as jnp
import numpy as np
from jax import lax
from jax.experimental import pallas as pl
from jax.experimental.pallas import tpu as pltpu
from jax.sharding import PartitionSpec as P

GX = 96
GXY = 9216
GZ = 32
DIRS = 2048
ORIENTS = 16
ORIENT_GRID = 16
THETA_GRID = 180
LANES = 128
CHUNK = 384
STEPS = GXY // CHUNK
PARTS = CHUNK // LANES
ROWS = CHUNK // GX
TILES = DIRS // LANES

wave_step = 0.4


def fit_even(function, count):
    nodes = np.cos((np.arange(400) + 0.5) * math.pi / 400)
    square = (nodes + 1.0) * (math.pi * math.pi / 2.0)
    series = np.polynomial.chebyshev.Chebyshev.fit(
        square, function(np.sqrt(square)), count - 1, domain=[0.0, math.pi * math.pi]
    )
    return [float(c) for c in series.convert(kind=np.polynomial.Polynomial).coef]


COS_FIT = fit_even(np.cos, 8)
SIN_FIT = fit_even(lambda r: np.sinc(r / math.pi), 8)


def cos_sin(angle):
    turns = jnp.round(angle * (0.5 / math.pi))
    rest = angle - turns * 6.28125
    rest = rest - turns * (2.0 * math.pi - 6.28125)
    square = rest * rest
    cosine = jnp.full_like(square, COS_FIT[-1])
    for c in COS_FIT[-2::-1]:
        cosine = cosine * square + c
    sine = jnp.full_like(square, SIN_FIT[-1])
    for c in SIN_FIT[-2::-1]:
        sine = sine * square + c
    return cosine, sine * rest


def times(a, b):
    return a[0] * b[0] - a[1] * b[1], a[0] * b[1] + a[1] * b[0]


def rows_of(shape):
    return lax.broadcasted_iota(jnp.int32, shape, 0)


def between(rows, first, count):
    return ((rows - first) & 7) < count


def sum_rows(tiles):
    rows = rows_of((8, LANES))
    by_four = []
    for k, first in ((3, 0), (1, 6), (2, 7), (0, 5)):
        mask = between(rows, first, 4)
        here, there = tiles[k], tiles[k + 4]
        by_four.append(
            jnp.where(mask, here, there) + pltpu.roll(jnp.where(mask, there, here), 4, 0)
        )
    by_two = []
    for k, first in ((0, 2), (2, 1)):
        mask = between(rows, first, 2) | between(rows, first + 4, 2)
        here, there = by_four[k], by_four[k + 1]
        by_two.append(
            jnp.where(mask, here, there) + pltpu.roll(jnp.where(mask, there, here), 2, 0)
        )
    mask = (rows & 1) == 1
    here, there = by_two
    return jnp.where(mask, here, there) + pltpu.roll(jnp.where(mask, there, here), 1, 0)


def make_table(tile, base, rows, target):
    start_re, start_im = base[0, 8 * tile : 8 * tile + 8, :], base[1, 8 * tile : 8 * tile + 8, :]
    y_re, y_im = rows[12, tile : tile + 1, :], rows[13, tile : tile + 1, :]
    strips = [None] * 12
    for k in range(6):
        turn_re, turn_im = rows[2 * k, tile : tile + 1, :], rows[2 * k + 1, tile : tile + 1, :]
        rr, ii, ri, ir = start_re * turn_re, start_im * turn_im, start_re * turn_im, start_im * turn_re
        strips[6 + k] = (rr - ii, ri + ir)
        strips[5 - k] = (rr + ii, ir - ri)
    twice = y_re + y_re
    for a in range(0, 12, 2):
        line = [[None, None] for _ in range(ROWS)]
        for k in range(2):
            v_re, v_im = strips[a + k]
            rr, ii, ri, ir = v_re * y_re, v_im * y_im, v_re * y_im, v_im * y_re
            after = (rr - ii, ri + ir)
            line[0][k] = (rr + ii, ir - ri)
            line[1][k] = (v_re, v_im)
            line[2][k] = after
            line[3][k] = (twice * after[0] - v_re, twice * after[1] - v_im)
        for y in range(ROWS):
            at = y * GX + 8 * a
            for part in range(2):
                value = jnp.concatenate([line[y][0][part], line[y][1][part]], axis=0)
                columns = slice(part * LANES, (part + 1) * LANES)
                target[at : at + 16, columns] = value.astype(jnp.bfloat16)


def finish(tile, table, lhs, rows, jump, out, place):
    half = lax.broadcasted_iota(jnp.int32, (8, LANES), 1) < LANES // 2
    product = jnp.dot(lhs[...], table[...], preferred_element_type=jnp.float32)
    jump_re = jump[0, STEPS * tile : STEPS * tile + STEPS, :].reshape(3, 8, LANES)
    jump_im = jump[1, STEPS * tile : STEPS * tile + STEPS, :].reshape(3, 8, LANES)
    sums = []
    for group in range(12):
        at = STEPS * group
        c = [product[at + 8 * h : at + 8 * h + 8, :LANES] for h in range(3)]
        s = [product[at + 8 * h : at + 8 * h + 8, LANES:] for h in range(3)]
        real = sum(c[h] * jump_re[h] for h in range(3)) - sum(s[h] * jump_im[h] for h in range(3))
        imag = sum(c[h] * jump_im[h] + s[h] * jump_re[h] for h in range(3))
        sums.append((real, imag))
    row = [rows[14 + k, tile : tile + 1, :] for k in range(10)]
    result = []
    for part in range(2):
        tiles = []
        for incident in range(2):
            for o in range(2):
                along = [sums[4 * c + 2 * incident + o][part] for c in range(3)]
                tiles.append(sum(along[c] * row[5 * o + c] for c in range(3)))
        for incident in (1, 0):
            for o in range(2):
                along = [sums[4 * c + 2 * incident + o][part] for c in range(2)]
                tiles.append(sum(along[c] * row[5 * o + 3 + c] for c in range(2)))
        result.append(sum_rows(tiles))
    real, imag = result
    out[2 * place] = jnp.where(half, real, pltpu.roll(imag, LANES // 2, 1))
    out[2 * place + 1] = jnp.where(half, pltpu.roll(real, LANES // 2, 1), imag)


def first_kernel(
    pol_hbm, occ_hbm, dirs_hbm, orients_hbm, out, lhs, rows, base, jump, following, pol, occ, dirs, orients, sems, polf, table
):
    copies = [
        pltpu.make_async_copy(source, target, sems.at[k])
        for k, (source, target) in enumerate(
            ((dirs_hbm, dirs), (orients_hbm, orients), (pol_hbm, pol), (occ_hbm, occ))
        )
    ]
    for copy in copies:
        copy.start()
    orient_rank = lax.axis_index("orient")
    core = lax.axis_index("core")
    plane = (2 * lax.axis_index("chip") + core).astype(jnp.float32)

    copies[0].wait()
    low_lanes = lax.broadcasted_iota(jnp.int32, (TILES // 2, LANES), 1) < LANES // 2

    def in_rows(first):
        even = dirs[pl.ds(first, TILES // 2, stride=4), :].astype(jnp.float32)
        odd = dirs[pl.ds(first + 2, TILES // 2, stride=4), :].astype(jnp.float32)
        of_core0 = jnp.where(low_lanes, even, pltpu.roll(odd, LANES // 2, 1))
        of_core1 = jnp.where(low_lanes, pltpu.roll(even, LANES // 2, 1), odd)
        here = jnp.where(core == 0, of_core0, of_core1)
        there = jnp.where(core == 0, of_core1, of_core0)
        return jnp.concatenate([there, here], axis=0)

    polar = (in_rows(0) + 0.5) * (math.pi / THETA_GRID)
    azimuth = in_rows(1) * (2.0 * math.pi / THETA_GRID)
    cos_polar, sin_polar = cos_sin(polar)
    cos_azimuth, sin_azimuth = cos_sin(azimuth)

    x1 = cos_sin(-wave_step * (sin_polar * cos_azimuth))
    y1 = cos_sin(-wave_step * (sin_polar * sin_azimuth))
    z = cos_sin(-wave_step * plane * cos_polar)
    x2 = times(x1, x1)
    x3 = times(x2, x1)
    x4 = times(x2, x2)
    x8 = times(x4, x4)
    fine = [None, x1, x2, x3, x4, times(x4, x1), times(x4, x2), times(x4, x3)]
    for k in range(8):
        value = times(z, fine[k]) if k else z
        for part in range(2):
            base[part, pl.ds(k, TILES, stride=8), :] = value[part]
    coarse = x4
    for k in range(6):
        rows[2 * k], rows[2 * k + 1] = coarse
        coarse = times(coarse, x8)
    rows[12], rows[13] = y1
    y2 = times(y1, y1)
    powers = [(jnp.ones_like(polar), jnp.zeros_like(polar)), times(y2, y2)]
    for k in range(2, STEPS):
        powers.append(times(powers[k // 2], powers[k - k // 2]))
    for k in range(STEPS):
        for part in range(2):
            jump[part, pl.ds(k, TILES, stride=STEPS), :] = powers[k][part]

    copies[1].wait()
    lane16 = lax.broadcasted_iota(jnp.int32, (1, ORIENTS), 1)
    turns = orients[0:1, :].astype(jnp.float32) * (2.0 * math.pi / ORIENT_GRID)
    weights = cos_sin((orients[1:2, :].astype(jnp.float32) + 0.5) * (math.pi / ORIENT_GRID))[1]
    shares = weights / (jnp.sum(weights, axis=1, keepdims=True) * float(GZ * GXY))
    for o in range(2):
        mine = lane16 == 2 * orient_rank + o
        turn = jnp.sum(jnp.where(mine, turns, 0.0), axis=1, keepdims=True)
        root = jnp.sqrt(jnp.sum(jnp.where(mine, shares, 0.0), axis=1, keepdims=True))
        cos_turn, sin_turn = cos_sin(azimuth - turn)
        cos_turn, sin_turn = cos_turn * root, sin_turn * root
        at = 14 + 5 * o
        rows[at] = cos_polar * cos_turn
        rows[at + 1] = cos_polar * sin_turn
        rows[at + 2] = -sin_polar * root
        rows[at + 3] = -sin_turn
        rows[at + 4] = cos_turn

    make_table(0, base, rows, table.at[0])

    for copy in copies[2:]:
        copy.wait()
    polf[...] = pol[...].astype(jnp.float32)
    for part in range(PARTS):
        mask = occ[pl.ds(part, STEPS, stride=PARTS), :].astype(jnp.float32)
        loaded = [
            polf[pl.ds(2 * part + incident, 6 * STEPS, stride=2 * PARTS), :].reshape(2, 3, STEPS, LANES)
            for incident in range(2)
        ]
        lhs[:, part * LANES : (part + 1) * LANES] = jnp.concatenate(
            [
                loaded[incident][o, c] * mask
                for c in range(3)
                for incident in range(2)
                for o in range(2)
            ],
            axis=0,
        ).astype(jnp.bfloat16)

    for tile in range(TILES // 2):
        after = table.at[(tile + 1) % 2] if tile + 1 < TILES // 2 else following
        make_table(tile + 1, base, rows, after)
        finish(tile, table.at[tile % 2], lhs, rows, jump, out, tile)


def second_kernel(lhs, rows, base, jump, started, out, table):
    for tile in range(TILES // 2, TILES):
        if tile + 1 < TILES:
            make_table(tile + 1, base, rows, table.at[(tile + 1) % 2])
        here = started if tile == TILES // 2 else table.at[tile % 2]
        finish(tile, here, lhs, rows, jump, out, tile - TILES // 2)


def add_kernel(a, b, out):
    out[...] = a[...] + b[...]


def mueller_kernel(parts, out):
    total = parts[0]
    for k in range(1, parts.shape[0]):
        total = total + parts[k]
    other = pltpu.roll(total, 4, 0)
    lane = lax.broadcasted_iota(jnp.int32, (8, LANES), 1)
    side = jnp.where(rows_of((8, LANES)) < 4, 0.5, -0.5)
    turned = pltpu.roll(other, LANES // 2, 1) * jnp.where(lane < LANES // 2, -side, side)
    square = total * total
    elements = [0.5 * square, side * square, 0.5 * (total * other), total * turned]
    final = sum_rows(elements + elements)
    for k in range(out.shape[0]):
        out[k] = final


def average_kernel(parts, out):
    total = parts[0]
    for k in range(1, parts.shape[0]):
        total = total + parts[k]
    total = total + pltpu.roll(total, LANES // 2, 1)
    out[...] = total[0:4, : LANES // 2]


VMEM = pl.BlockSpec(memory_space=pltpu.VMEM)
HBM = pl.BlockSpec(memory_space=pltpu.HBM)


def in_vmem(arrays):
    return [pltpu.with_memory_space_constraint(x, pltpu.VMEM) for x in arrays]


def amplitudes(polarization, occupied, orient_table, dir_index):
    pol = polarization.transpose(0, 2, 3, 1, 4).reshape(6, 2, GXY // LANES, LANES)
    pol = pol.transpose(0, 2, 1, 3).reshape(12 * GXY // LANES, LANES)
    occ = occupied.reshape(GXY // LANES, LANES)
    dirs = dir_index.T.reshape(2, TILES, LANES).transpose(1, 0, 2).reshape(2 * TILES, LANES)
    operands = (pol, occ, dirs, orient_table.T)
    block = pltpu.VMEM((TILES, 8, LANES), jnp.float32)
    there, *kept = pl.pallas_call(
        first_kernel,
        out_shape=(
            block,
            pltpu.VMEM((12 * STEPS, CHUNK), jnp.bfloat16),
            pltpu.VMEM((24, TILES, LANES), jnp.float32),
            pltpu.VMEM((2, 8 * TILES, LANES), jnp.float32),
            pltpu.VMEM((2, STEPS * TILES, LANES), jnp.float32),
            pltpu.VMEM((CHUNK, 2 * LANES), jnp.bfloat16),
        ),
        in_specs=[HBM] * 4,
        out_specs=(VMEM,) * 6,
        scratch_shapes=[pltpu.VMEM(x.shape, x.dtype) for x in operands]
        + [
            pltpu.SemaphoreType.DMA((4,)),
            pltpu.VMEM(pol.shape, jnp.float32),
            pltpu.VMEM((2, CHUNK, 2 * LANES), jnp.bfloat16),
        ],
        compiler_params=pltpu.CompilerParams(vmem_limit_bytes=24 << 20),
        name="amplitude_first",
    )(*(pltpu.with_memory_space_constraint(x, pltpu.HBM) for x in operands))
    received = lax.ppermute(there, "core", [(0, 1), (1, 0)])
    here = pl.pallas_call(
        second_kernel,
        out_shape=block,
        in_specs=[VMEM] * 5,
        out_specs=VMEM,
        scratch_shapes=[pltpu.VMEM((2, CHUNK, 2 * LANES), jnp.bfloat16)],
        compiler_params=pltpu.CompilerParams(vmem_limit_bytes=24 << 20),
        cost_estimate=pl.CostEstimate(
            flops=12 * GXY * 2 * DIRS, bytes_accessed=1 << 20, transcendentals=0
        ),
        name="amplitude_second",
    )(*in_vmem(kept))
    return pl.pallas_call(
        add_kernel, out_shape=block, in_specs=[VMEM] * 2, out_specs=VMEM, name="add"
    )(*in_vmem((here, received)))


def shards(polarization, occupied, orient_table, dir_index):
    amplitude = amplitudes(polarization, occupied, orient_table, dir_index)
    parts = lax.all_to_all(amplitude, "chip", 0, 0, tiled=True)
    copies = pl.pallas_call(
        mueller_kernel,
        out_shape=pltpu.VMEM((lax.axis_size("orient"), 8, LANES), jnp.float32),
        in_specs=[VMEM],
        out_specs=VMEM,
        name="mueller",
    )(*in_vmem((parts,)))
    parts = lax.all_to_all(copies, "orient", 0, 0, tiled=True)
    return pl.pallas_call(
        average_kernel,
        out_shape=jax.ShapeDtypeStruct((4, LANES // 2), jnp.float32),
        in_specs=[VMEM],
        out_specs=VMEM,
        name="average",
    )(*in_vmem((parts,)))


def solution(mesh):
    slab = ("chip", "core")
    return jax.shard_map(
        shards,
        mesh=jax.sharding.Mesh(mesh.devices.reshape(8, 16, 2), ("orient", *slab)),
        in_specs=(P("orient", None, None, slab, None), P(slab, None), P(), P()),
        out_specs=P(None, slab),
        check_vma=False,
    )
```

```python
import functools
import math

import jax
import jax.numpy as jnp
import numpy as np
from jax import lax
from jax.experimental import pallas as pl
from jax.experimental.pallas import tpu as pltpu
from jax.sharding import PartitionSpec as P

GX = 96
GXY = 9216
GZ = 32
DIRS = 2048
ORIENTS = 16
ORIENT_GRID = 16
THETA_GRID = 180
LANES = 128
CHUNK = 384
STEPS = GXY // CHUNK
PARTS = CHUNK // LANES
ROWS = CHUNK // GX
TILES = DIRS // LANES
CHIPS = 16
FIRST_CHIP = 10
FIRST_ORIENT = 4

wave_step = 0.4


def fit_even(function, count):
    nodes = np.cos((np.arange(400) + 0.5) * math.pi / 400)
    square = (nodes + 1.0) * (math.pi * math.pi / 2.0)
    series = np.polynomial.chebyshev.Chebyshev.fit(
        square, function(np.sqrt(square)), count - 1, domain=[0.0, math.pi * math.pi]
    )
    return [float(c) for c in series.convert(kind=np.polynomial.Polynomial).coef]


COS_FIT = fit_even(np.cos, 8)
SIN_FIT = fit_even(lambda r: np.sinc(r / math.pi), 8)


def cos_sin(angle):
    turns = jnp.round(angle * (0.5 / math.pi))
    rest = angle - turns * 6.28125
    rest = rest - turns * (2.0 * math.pi - 6.28125)
    square = rest * rest
    cosine = jnp.full_like(square, COS_FIT[-1])
    for c in COS_FIT[-2::-1]:
        cosine = cosine * square + c
    sine = jnp.full_like(square, SIN_FIT[-1])
    for c in SIN_FIT[-2::-1]:
        sine = sine * square + c
    return cosine, sine * rest


def times(a, b):
    return a[0] * b[0] - a[1] * b[1], a[0] * b[1] + a[1] * b[0]


def rows_of(shape):
    return lax.broadcasted_iota(jnp.int32, shape, 0)


def between(rows, first, count):
    return ((rows - first) & 7) < count


def sum_rows(tiles):
    rows = rows_of((8, LANES))
    by_four = []
    for k, first in ((3, 0), (1, 6), (2, 7), (0, 5)):
        mask = between(rows, first, 4)
        here, there = tiles[k], tiles[k + 4]
        by_four.append(
            jnp.where(mask, here, there) + pltpu.roll(jnp.where(mask, there, here), 4, 0)
        )
    by_two = []
    for k, first in ((0, 2), (2, 1)):
        mask = between(rows, first, 2) | between(rows, first + 4, 2)
        here, there = by_four[k], by_four[k + 1]
        by_two.append(
            jnp.where(mask, here, there) + pltpu.roll(jnp.where(mask, there, here), 2, 0)
        )
    mask = (rows & 1) == 1
    here, there = by_two
    return jnp.where(mask, here, there) + pltpu.roll(jnp.where(mask, there, here), 1, 0)


def make_table(tile, base, rows, target):
    start_re, start_im = base[0, 8 * tile : 8 * tile + 8, :], base[1, 8 * tile : 8 * tile + 8, :]
    y_re, y_im = rows[12, tile : tile + 1, :], rows[13, tile : tile + 1, :]
    strips = [None] * 12
    for k in range(6):
        turn_re, turn_im = rows[2 * k, tile : tile + 1, :], rows[2 * k + 1, tile : tile + 1, :]
        rr, ii, ri, ir = start_re * turn_re, start_im * turn_im, start_re * turn_im, start_im * turn_re
        strips[6 + k] = (rr - ii, ri + ir)
        strips[5 - k] = (rr + ii, ir - ri)
    twice = y_re + y_re
    for a in range(0, 12, 2):
        line = [[None, None] for _ in range(ROWS)]
        for k in range(2):
            v_re, v_im = strips[a + k]
            rr, ii, ri, ir = v_re * y_re, v_im * y_im, v_re * y_im, v_im * y_re
            after = (rr - ii, ri + ir)
            line[0][k] = (rr + ii, ir - ri)
            line[1][k] = (v_re, v_im)
            line[2][k] = after
            line[3][k] = (twice * after[0] - v_re, twice * after[1] - v_im)
        for y in range(ROWS):
            at = y * GX + 8 * a
            for part in range(2):
                value = jnp.concatenate([line[y][0][part], line[y][1][part]], axis=0)
                columns = slice(part * LANES, (part + 1) * LANES)
                target[at : at + 16, columns] = value.astype(jnp.bfloat16)


def finish(tile, table, lhs, rows, jump, out, place):
    half = lax.broadcasted_iota(jnp.int32, (8, LANES), 1) < LANES // 2
    product = jnp.dot(lhs[...], table[...], preferred_element_type=jnp.float32)
    jump_re = jump[0, STEPS * tile : STEPS * tile + STEPS, :].reshape(3, 8, LANES)
    jump_im = jump[1, STEPS * tile : STEPS * tile + STEPS, :].reshape(3, 8, LANES)
    sums = []
    for group in range(12):
        at = STEPS * group
        c = [product[at + 8 * h : at + 8 * h + 8, :LANES] for h in range(3)]
        s = [product[at + 8 * h : at + 8 * h + 8, LANES:] for h in range(3)]
        real = sum(c[h] * jump_re[h] for h in range(3)) - sum(s[h] * jump_im[h] for h in range(3))
        imag = sum(c[h] * jump_im[h] + s[h] * jump_re[h] for h in range(3))
        sums.append((real, imag))
    row = [rows[14 + k, tile : tile + 1, :] for k in range(10)]
    result = []
    for part in range(2):
        tiles = []
        for incident in range(2):
            for o in range(2):
                along = [sums[4 * c + 2 * incident + o][part] for c in range(3)]
                tiles.append(sum(along[c] * row[5 * o + c] for c in range(3)))
        for incident in (1, 0):
            for o in range(2):
                along = [sums[4 * c + 2 * incident + o][part] for c in range(2)]
                tiles.append(sum(along[c] * row[5 * o + 3 + c] for c in range(2)))
        result.append(sum_rows(tiles))
    real, imag = result
    at = (2 * place - FIRST_CHIP) % CHIPS
    out[at] = jnp.where(half, real, pltpu.roll(imag, LANES // 2, 1))
    out[(at + 1) % CHIPS] = jnp.where(half, pltpu.roll(real, LANES // 2, 1), imag)


def first_kernel(
    pol_hbm, occ_hbm, dirs_hbm, orients_hbm, out, lhs, rows, base, jump, following, pol, occ, dirs, orients, sems, polf, table
):
    copies = [
        pltpu.make_async_copy(source, target, sems.at[k])
        for k, (source, target) in enumerate(
            ((dirs_hbm, dirs), (orients_hbm, orients), (pol_hbm, pol), (occ_hbm, occ))
        )
    ]
    for copy in copies:
        copy.start()
    orient_rank = lax.axis_index("orient")
    core = lax.axis_index("core")
    plane = (2 * lax.axis_index("chip") + core).astype(jnp.float32)

    copies[0].wait()
    low_lanes = lax.broadcasted_iota(jnp.int32, (TILES // 2, LANES), 1) < LANES // 2

    def in_rows(first):
        even = dirs[pl.ds(first, TILES // 2, stride=4), :].astype(jnp.float32)
        odd = dirs[pl.ds(first + 2, TILES // 2, stride=4), :].astype(jnp.float32)
        of_core0 = jnp.where(low_lanes, even, pltpu.roll(odd, LANES // 2, 1))
        of_core1 = jnp.where(low_lanes, pltpu.roll(even, LANES // 2, 1), odd)
        here = jnp.where(core == 0, of_core0, of_core1)
        there = jnp.where(core == 0, of_core1, of_core0)
        return jnp.concatenate([there, here], axis=0)

    polar = (in_rows(0) + 0.5) * (math.pi / THETA_GRID)
    azimuth = in_rows(1) * (2.0 * math.pi / THETA_GRID)
    cos_polar, sin_polar = cos_sin(polar)
    cos_azimuth, sin_azimuth = cos_sin(azimuth)

    x1 = cos_sin(-wave_step * (sin_polar * cos_azimuth))
    y1 = cos_sin(-wave_step * (sin_polar * sin_azimuth))
    z = cos_sin(-wave_step * plane * cos_polar)
    x2 = times(x1, x1)
    x3 = times(x2, x1)
    x4 = times(x2, x2)
    x8 = times(x4, x4)
    fine = [None, x1, x2, x3, x4, times(x4, x1), times(x4, x2), times(x4, x3)]
    for k in range(8):
        value = times(z, fine[k]) if k else z
        for part in range(2):
            base[part, pl.ds(k, TILES, stride=8), :] = value[part]
    coarse = x4
    for k in range(6):
        rows[2 * k], rows[2 * k + 1] = coarse
        coarse = times(coarse, x8)
    rows[12], rows[13] = y1
    y2 = times(y1, y1)
    powers = [(jnp.ones_like(polar), jnp.zeros_like(polar)), times(y2, y2)]
    for k in range(2, STEPS):
        powers.append(times(powers[k // 2], powers[k - k // 2]))
    for k in range(STEPS):
        for part in range(2):
            jump[part, pl.ds(k, TILES, stride=STEPS), :] = powers[k][part]

    copies[1].wait()
    lane16 = lax.broadcasted_iota(jnp.int32, (1, ORIENTS), 1)
    turns = orients[0:1, :].astype(jnp.float32) * (2.0 * math.pi / ORIENT_GRID)
    weights = cos_sin((orients[1:2, :].astype(jnp.float32) + 0.5) * (math.pi / ORIENT_GRID))[1]
    shares = weights / (jnp.sum(weights, axis=1, keepdims=True) * float(GZ * GXY))
    for o in range(2):
        mine = lane16 == 2 * orient_rank + o
        turn = jnp.sum(jnp.where(mine, turns, 0.0), axis=1, keepdims=True)
        root = jnp.sqrt(jnp.sum(jnp.where(mine, shares, 0.0), axis=1, keepdims=True))
        cos_turn, sin_turn = cos_sin(azimuth - turn)
        cos_turn, sin_turn = cos_turn * root, sin_turn * root
        at = 14 + 5 * o
        rows[at] = cos_polar * cos_turn
        rows[at + 1] = cos_polar * sin_turn
        rows[at + 2] = -sin_polar * root
        rows[at + 3] = -sin_turn
        rows[at + 4] = cos_turn

    make_table(0, base, rows, table.at[0])

    for copy in copies[2:]:
        copy.wait()
    polf[...] = pol[...].astype(jnp.float32)
    for part in range(PARTS):
        mask = occ[pl.ds(part, STEPS, stride=PARTS), :].astype(jnp.float32)
        loaded = [
            polf[pl.ds(2 * part + incident, 6 * STEPS, stride=2 * PARTS), :].reshape(2, 3, STEPS, LANES)
            for incident in range(2)
        ]
        lhs[:, part * LANES : (part + 1) * LANES] = jnp.concatenate(
            [
                loaded[incident][o, c] * mask
                for c in range(3)
                for incident in range(2)
                for o in range(2)
            ],
            axis=0,
        ).astype(jnp.bfloat16)

    for tile in range(TILES // 2):
        after = table.at[(tile + 1) % 2] if tile + 1 < TILES // 2 else following
        make_table(tile + 1, base, rows, after)
        finish(tile, table.at[tile % 2], lhs, rows, jump, out, tile)


def second_kernel(lhs, rows, base, jump, started, out, table):
    for tile in range(TILES // 2, TILES):
        if tile + 1 < TILES:
            make_table(tile + 1, base, rows, table.at[(tile + 1) % 2])
        here = started if tile == TILES // 2 else table.at[tile % 2]
        finish(tile, here, lhs, rows, jump, out, tile - TILES // 2)


def add_kernel(a, b, out):
    out[...] = a[...] + b[...]


def mueller_kernel(parts, out):
    total = parts[0]
    for k in range(1, parts.shape[0]):
        total = total + parts[k]
    other = pltpu.roll(total, 4, 0)
    lane = lax.broadcasted_iota(jnp.int32, (8, LANES), 1)
    side = jnp.where(rows_of((8, LANES)) < 4, 0.5, -0.5)
    turned = pltpu.roll(other, LANES // 2, 1) * jnp.where(lane < LANES // 2, -side, side)
    square = total * total
    elements = [0.5 * square, side * square, 0.5 * (total * other), total * turned]
    final = sum_rows(elements + elements)
    for k in range(out.shape[0]):
        out[k] = final


def average_kernel(parts, out):
    total = parts[0]
    for k in range(1, parts.shape[0]):
        total = total + parts[k]
    total = total + pltpu.roll(total, LANES // 2, 1)
    out[...] = total[0:4, : LANES // 2]


VMEM = pl.BlockSpec(memory_space=pltpu.VMEM)
HBM = pl.BlockSpec(memory_space=pltpu.HBM)


def in_vmem(arrays):
    return [pltpu.with_memory_space_constraint(x, pltpu.VMEM) for x in arrays]


def exchange(blocks, axis, first):
    size = lax.axis_size(axis)
    group = [(first + k) % size for k in range(size)]
    return lax.all_to_all(blocks, axis, 0, 0, tiled=True, axis_index_groups=[group])


def amplitudes(polarization, occupied, orient_table, dir_index):
    pol = polarization.transpose(0, 2, 3, 1, 4).reshape(6, 2, GXY // LANES, LANES)
    pol = pol.transpose(0, 2, 1, 3).reshape(12 * GXY // LANES, LANES)
    occ = occupied.reshape(GXY // LANES, LANES)
    dirs = dir_index.T.reshape(2, TILES, LANES).transpose(1, 0, 2).reshape(2 * TILES, LANES)
    operands = (pol, occ, dirs, orient_table.T)
    block = pltpu.VMEM((TILES, 8, LANES), jnp.float32)
    there, *kept = pl.pallas_call(
        first_kernel,
        out_shape=(
            block,
            pltpu.VMEM((12 * STEPS, CHUNK), jnp.bfloat16),
            pltpu.VMEM((24, TILES, LANES), jnp.float32),
            pltpu.VMEM((2, 8 * TILES, LANES), jnp.float32),
            pltpu.VMEM((2, STEPS * TILES, LANES), jnp.float32),
            pltpu.VMEM((CHUNK, 2 * LANES), jnp.bfloat16),
        ),
        in_specs=[HBM] * 4,
        out_specs=(VMEM,) * 6,
        scratch_shapes=[pltpu.VMEM(x.shape, x.dtype) for x in operands]
        + [
            pltpu.SemaphoreType.DMA((4,)),
            pltpu.VMEM(pol.shape, jnp.float32),
            pltpu.VMEM((2, CHUNK, 2 * LANES), jnp.bfloat16),
        ],
        compiler_params=pltpu.CompilerParams(vmem_limit_bytes=24 << 20),
        name="amplitude_first",
    )(*(pltpu.with_memory_space_constraint(x, pltpu.HBM) for x in operands))
    received = lax.ppermute(there, "core", [(0, 1), (1, 0)])
    here = pl.pallas_call(
        second_kernel,
        out_shape=block,
        in_specs=[VMEM] * 5,
        out_specs=VMEM,
        scratch_shapes=[pltpu.VMEM((2, CHUNK, 2 * LANES), jnp.bfloat16)],
        compiler_params=pltpu.CompilerParams(vmem_limit_bytes=24 << 20),
        cost_estimate=pl.CostEstimate(
            flops=12 * GXY * 2 * DIRS, bytes_accessed=1 << 20, transcendentals=0
        ),
        name="amplitude_second",
    )(*in_vmem(kept))
    return pl.pallas_call(
        add_kernel, out_shape=block, in_specs=[VMEM] * 2, out_specs=VMEM, name="add"
    )(*in_vmem((here, received)))


def shards(polarization, occupied, orient_table, dir_index):
    amplitude = amplitudes(polarization, occupied, orient_table, dir_index)
    parts = exchange(amplitude, "chip", FIRST_CHIP)
    copies = pl.pallas_call(
        mueller_kernel,
        out_shape=pltpu.VMEM((lax.axis_size("orient"), 8, LANES), jnp.float32),
        in_specs=[VMEM],
        out_specs=VMEM,
        name="mueller",
    )(*in_vmem((parts,)))
    parts = exchange(copies, "orient", FIRST_ORIENT)
    return pl.pallas_call(
        average_kernel,
        out_shape=jax.ShapeDtypeStruct((4, LANES // 2), jnp.float32),
        in_specs=[VMEM],
        out_specs=VMEM,
        name="average",
    )(*in_vmem((parts,)))


def solution(mesh):
    slab = ("chip", "core")
    return jax.shard_map(
        shards,
        mesh=jax.sharding.Mesh(mesh.devices.reshape(8, 16, 2), ("orient", *slab)),
        in_specs=(P("orient", None, None, slab, None), P(slab, None), P(), P()),
        out_specs=P(None, slab),
        check_vma=False,
    )
```

```python
import functools
import math

import jax
import jax.numpy as jnp
import numpy as np
from jax import lax
from jax.experimental import pallas as pl
from jax.experimental.pallas import tpu as pltpu
from jax.sharding import PartitionSpec as P

GX = 96
GXY = 9216
GZ = 32
DIRS = 2048
ORIENTS = 16
ORIENT_GRID = 16
THETA_GRID = 180
LANES = 128
CHUNK = 384
STEPS = GXY // CHUNK
PARTS = CHUNK // LANES
ROWS = CHUNK // GX
TILES = DIRS // LANES
SLABS = 32
FIRST_SLAB = 21
FIRST_ORIENT = 4

wave_step = 0.4


def fit_even(function, count):
    nodes = np.cos((np.arange(400) + 0.5) * math.pi / 400)
    square = (nodes + 1.0) * (math.pi * math.pi / 2.0)
    series = np.polynomial.chebyshev.Chebyshev.fit(
        square, function(np.sqrt(square)), count - 1, domain=[0.0, math.pi * math.pi]
    )
    return [float(c) for c in series.convert(kind=np.polynomial.Polynomial).coef]


COS_FIT = fit_even(np.cos, 8)
SIN_FIT = fit_even(lambda r: np.sinc(r / math.pi), 8)


def cos_sin(angle):
    turns = jnp.round(angle * (0.5 / math.pi))
    rest = angle - turns * 6.28125
    rest = rest - turns * (2.0 * math.pi - 6.28125)
    square = rest * rest
    cosine = jnp.full_like(square, COS_FIT[-1])
    for c in COS_FIT[-2::-1]:
        cosine = cosine * square + c
    sine = jnp.full_like(square, SIN_FIT[-1])
    for c in SIN_FIT[-2::-1]:
        sine = sine * square + c
    return cosine, sine * rest


def times(a, b):
    return a[0] * b[0] - a[1] * b[1], a[0] * b[1] + a[1] * b[0]


def rows_of(shape):
    return lax.broadcasted_iota(jnp.int32, shape, 0)


def between(rows, first, count):
    return ((rows - first) & 7) < count


def sum_rows(tiles):
    rows = rows_of((8, LANES))
    by_four = []
    for k, first in ((3, 0), (1, 6), (2, 7), (0, 5)):
        mask = between(rows, first, 4)
        here, there = tiles[k], tiles[k + 4]
        by_four.append(
            jnp.where(mask, here, there) + pltpu.roll(jnp.where(mask, there, here), 4, 0)
        )
    by_two = []
    for k, first in ((0, 2), (2, 1)):
        mask = between(rows, first, 2) | between(rows, first + 4, 2)
        here, there = by_four[k], by_four[k + 1]
        by_two.append(
            jnp.where(mask, here, there) + pltpu.roll(jnp.where(mask, there, here), 2, 0)
        )
    mask = (rows & 1) == 1
    here, there = by_two
    return jnp.where(mask, here, there) + pltpu.roll(jnp.where(mask, there, here), 1, 0)


def amplitude_kernel(
    pol_hbm, occ_hbm, dirs_hbm, orients_hbm, out, pol, occ, dirs, orients, sems, polf, lhs, rows, base, jump, table
):
    copies = [
        pltpu.make_async_copy(source, target, sems.at[k])
        for k, (source, target) in enumerate(
            ((dirs_hbm, dirs), (orients_hbm, orients), (pol_hbm, pol), (occ_hbm, occ))
        )
    ]
    for copy in copies:
        copy.start()
    orient_rank = lax.axis_index("orient")
    slab_rank = lax.axis_index("slab")
    plane = slab_rank.astype(jnp.float32)

    copies[0].wait()
    polar = (dirs[pl.ds(0, TILES, stride=2), :].astype(jnp.float32) + 0.5) * (math.pi / THETA_GRID)
    azimuth = dirs[pl.ds(1, TILES, stride=2), :].astype(jnp.float32) * (2.0 * math.pi / THETA_GRID)
    cos_polar, sin_polar = cos_sin(polar)
    cos_azimuth, sin_azimuth = cos_sin(azimuth)

    x1 = cos_sin(-wave_step * (sin_polar * cos_azimuth))
    y1 = cos_sin(-wave_step * (sin_polar * sin_azimuth))
    z = cos_sin(-wave_step * plane * cos_polar)
    x2 = times(x1, x1)
    x3 = times(x2, x1)
    x4 = times(x2, x2)
    x8 = times(x4, x4)
    fine = [None, x1, x2, x3, x4, times(x4, x1), times(x4, x2), times(x4, x3)]
    for k in range(8):
        value = times(z, fine[k]) if k else z
        for part in range(2):
            base[part, pl.ds(k, TILES, stride=8), :] = value[part]
    coarse = x4
    for k in range(6):
        rows[2 * k], rows[2 * k + 1] = coarse
        coarse = times(coarse, x8)
    rows[12], rows[13] = y1
    y2 = times(y1, y1)
    powers = [(jnp.ones_like(polar), jnp.zeros_like(polar)), times(y2, y2)]
    for k in range(2, STEPS):
        powers.append(times(powers[k // 2], powers[k - k // 2]))
    for k in range(STEPS):
        for part in range(2):
            jump[part, pl.ds(k, TILES, stride=STEPS), :] = powers[k][part]

    copies[1].wait()
    lane16 = lax.broadcasted_iota(jnp.int32, (1, ORIENTS), 1)
    turns = orients[0:1, :].astype(jnp.float32) * (2.0 * math.pi / ORIENT_GRID)
    weights = cos_sin((orients[1:2, :].astype(jnp.float32) + 0.5) * (math.pi / ORIENT_GRID))[1]
    shares = weights / (jnp.sum(weights, axis=1, keepdims=True) * float(GZ * GXY))
    for o in range(2):
        mine = lane16 == 2 * orient_rank + o
        turn = jnp.sum(jnp.where(mine, turns, 0.0), axis=1, keepdims=True)
        root = jnp.sqrt(jnp.sum(jnp.where(mine, shares, 0.0), axis=1, keepdims=True))
        cos_turn, sin_turn = cos_sin(azimuth - turn)
        cos_turn, sin_turn = cos_turn * root, sin_turn * root
        at = 14 + 5 * o
        rows[at] = cos_polar * cos_turn
        rows[at + 1] = cos_polar * sin_turn
        rows[at + 2] = -sin_polar * root
        rows[at + 3] = -sin_turn
        rows[at + 4] = cos_turn

    half = lax.broadcasted_iota(jnp.int32, (8, LANES), 1) < LANES // 2

    def make_table(tile, slot):
        start_re, start_im = base[0, 8 * tile : 8 * tile + 8, :], base[1, 8 * tile : 8 * tile + 8, :]
        y_re, y_im = rows[12, tile : tile + 1, :], rows[13, tile : tile + 1, :]
        strips = [None] * 12
        for k in range(6):
            turn_re, turn_im = rows[2 * k, tile : tile + 1, :], rows[2 * k + 1, tile : tile + 1, :]
            rr, ii, ri, ir = start_re * turn_re, start_im * turn_im, start_re * turn_im, start_im * turn_re
            strips[6 + k] = (rr - ii, ri + ir)
            strips[5 - k] = (rr + ii, ir - ri)
        twice = y_re + y_re
        for a in range(0, 12, 2):
            line = [[None, None] for _ in range(ROWS)]
            for k in range(2):
                v_re, v_im = strips[a + k]
                rr, ii, ri, ir = v_re * y_re, v_im * y_im, v_re * y_im, v_im * y_re
                after = (rr - ii, ri + ir)
                line[0][k] = (rr + ii, ir - ri)
                line[1][k] = (v_re, v_im)
                line[2][k] = after
                line[3][k] = (twice * after[0] - v_re, twice * after[1] - v_im)
            for y in range(ROWS):
                at = y * GX + 8 * a
                for part in range(2):
                    value = jnp.concatenate([line[y][0][part], line[y][1][part]], axis=0)
                    columns = slice(part * LANES, (part + 1) * LANES)
                    table[slot, at : at + 16, columns] = value.astype(jnp.bfloat16)

    def finish(tile, slot):
        product = jnp.dot(lhs[...], table[slot], preferred_element_type=jnp.float32)
        jump_re = jump[0, STEPS * tile : STEPS * tile + STEPS, :].reshape(3, 8, LANES)
        jump_im = jump[1, STEPS * tile : STEPS * tile + STEPS, :].reshape(3, 8, LANES)
        sums = []
        for group in range(12):
            at = STEPS * group
            c = [product[at + 8 * h : at + 8 * h + 8, :LANES] for h in range(3)]
            s = [product[at + 8 * h : at + 8 * h + 8, LANES:] for h in range(3)]
            real = sum(c[h] * jump_re[h] for h in range(3)) - sum(s[h] * jump_im[h] for h in range(3))
            imag = sum(c[h] * jump_im[h] + s[h] * jump_re[h] for h in range(3))
            sums.append((real, imag))
        row = [rows[14 + k, tile : tile + 1, :] for k in range(10)]
        result = []
        for part in range(2):
            tiles = []
            for incident in range(2):
                for o in range(2):
                    along = [sums[4 * c + 2 * incident + o][part] for c in range(3)]
                    tiles.append(sum(along[c] * row[5 * o + c] for c in range(3)))
            for incident in (1, 0):
                for o in range(2):
                    along = [sums[4 * c + 2 * incident + o][part] for c in range(2)]
                    tiles.append(sum(along[c] * row[5 * o + 3 + c] for c in range(2)))
            result.append(sum_rows(tiles))
        real, imag = result
        out[(2 * tile - FIRST_SLAB) % SLABS] = jnp.where(half, real, pltpu.roll(imag, LANES // 2, 1))
        out[(2 * tile + 1 - FIRST_SLAB) % SLABS] = jnp.where(half, pltpu.roll(real, LANES // 2, 1), imag)

    make_table(0, 0)

    for copy in copies[2:]:
        copy.wait()
    polf[...] = pol[...].astype(jnp.float32)
    for part in range(PARTS):
        mask = occ[pl.ds(part, STEPS, stride=PARTS), :].astype(jnp.float32)
        loaded = [
            polf[pl.ds(2 * part + incident, 6 * STEPS, stride=2 * PARTS), :].reshape(2, 3, STEPS, LANES)
            for incident in range(2)
        ]
        lhs[:, part * LANES : (part + 1) * LANES] = jnp.concatenate(
            [
                loaded[incident][o, c] * mask
                for c in range(3)
                for incident in range(2)
                for o in range(2)
            ],
            axis=0,
        ).astype(jnp.bfloat16)

    for tile in range(TILES):
        if tile + 1 < TILES:
            make_table(tile + 1, (tile + 1) % 2)
        finish(tile, tile % 2)


def mueller_kernel(parts, out):
    total = parts[0]
    for k in range(1, GZ):
        total = total + parts[k]
    other = pltpu.roll(total, 4, 0)
    lane = lax.broadcasted_iota(jnp.int32, (8, LANES), 1)
    side = jnp.where(rows_of((8, LANES)) < 4, 0.5, -0.5)
    turned = pltpu.roll(other, LANES // 2, 1) * jnp.where(lane < LANES // 2, -side, side)
    square = total * total
    elements = [0.5 * square, side * square, 0.5 * (total * other), total * turned]
    final = sum_rows(elements + elements)
    for k in range(out.shape[0]):
        out[k] = final


def average_kernel(parts, out):
    total = parts[0]
    for k in range(1, parts.shape[0]):
        total = total + parts[k]
    total = total + pltpu.roll(total, LANES // 2, 1)
    out[...] = total[0:4, : LANES // 2]


VMEM = pl.BlockSpec(memory_space=pltpu.VMEM)
HBM = pl.BlockSpec(memory_space=pltpu.HBM)


def exchange(blocks, axis, first):
    size = lax.axis_size(axis)
    group = [(first + k) % size for k in range(size)]
    return lax.all_to_all(blocks, axis, 0, 0, tiled=True, axis_index_groups=[group])


def amplitudes(polarization, occupied, orient_table, dir_index):
    pol = polarization.transpose(0, 2, 3, 1, 4).reshape(6, 2, GXY // LANES, LANES)
    pol = pol.transpose(0, 2, 1, 3).reshape(12 * GXY // LANES, LANES)
    occ = occupied.reshape(GXY // LANES, LANES)
    dirs = dir_index.T.reshape(2, TILES, LANES).transpose(1, 0, 2).reshape(2 * TILES, LANES)
    operands = (pol, occ, dirs, orient_table.T)
    return pl.pallas_call(
        amplitude_kernel,
        out_shape=pltpu.VMEM((GZ, 8, LANES), jnp.float32),
        in_specs=[HBM] * 4,
        out_specs=VMEM,
        scratch_shapes=[pltpu.VMEM(x.shape, x.dtype) for x in operands]
        + [
            pltpu.SemaphoreType.DMA((4,)),
            pltpu.VMEM(pol.shape, jnp.float32),
            pltpu.VMEM((12 * STEPS, CHUNK), jnp.bfloat16),
            pltpu.VMEM((24, TILES, LANES), jnp.float32),
            pltpu.VMEM((2, 8 * TILES, LANES), jnp.float32),
            pltpu.VMEM((2, STEPS * TILES, LANES), jnp.float32),
            pltpu.VMEM((2, CHUNK, 2 * LANES), jnp.bfloat16),
        ],
        compiler_params=pltpu.CompilerParams(vmem_limit_bytes=24 << 20),
        name="amplitude",
    )(*(pltpu.with_memory_space_constraint(x, pltpu.HBM) for x in operands))


def shards(polarization, occupied, orient_table, dir_index):
    amplitude = amplitudes(polarization, occupied, orient_table, dir_index)
    parts = exchange(amplitude, "slab", FIRST_SLAB)
    copies = pl.pallas_call(
        mueller_kernel,
        out_shape=pltpu.VMEM((lax.axis_size("orient"), 8, LANES), jnp.float32),
        in_specs=[VMEM],
        out_specs=VMEM,
        name="mueller",
    )(pltpu.with_memory_space_constraint(parts, pltpu.VMEM))
    parts = exchange(copies, "orient", FIRST_ORIENT)
    return pl.pallas_call(
        average_kernel,
        out_shape=jax.ShapeDtypeStruct((4, LANES // 2), jnp.float32),
        in_specs=[VMEM],
        out_specs=VMEM,
        name="average",
    )(pltpu.with_memory_space_constraint(parts, pltpu.VMEM))


def solution(mesh):
    return jax.shard_map(
        shards,
        mesh=mesh,
        in_specs=(P("orient", None, None, "slab", None), P("slab", None), P(), P()),
        out_specs=P(None, "slab"),
        check_vma=False,
    )
```

```python
import functools
import math

import jax
import jax.numpy as jnp
import numpy as np
from jax import lax
from jax.experimental import pallas as pl
from jax.experimental.pallas import tpu as pltpu
from jax.sharding import PartitionSpec as P

GX = 96
GXY = 9216
GZ = 32
DIRS = 2048
ORIENTS = 16
ORIENT_GRID = 16
THETA_GRID = 180
LANES = 128
CHUNK = 384
STEPS = GXY // CHUNK
PARTS = CHUNK // LANES
ROWS = CHUNK // GX
TILES = DIRS // LANES
SLABS = 32
FIRST_SLAB = 21
FIRST_ORIENT = 4

wave_step = 0.4


def fit_even(function, count):
    nodes = np.cos((np.arange(400) + 0.5) * math.pi / 400)
    square = (nodes + 1.0) * (math.pi * math.pi / 2.0)
    series = np.polynomial.chebyshev.Chebyshev.fit(
        square, function(np.sqrt(square)), count - 1, domain=[0.0, math.pi * math.pi]
    )
    return [float(c) for c in series.convert(kind=np.polynomial.Polynomial).coef]


COS_FIT = fit_even(np.cos, 8)
SIN_FIT = fit_even(lambda r: np.sinc(r / math.pi), 8)


def cos_sin(angle):
    turns = jnp.round(angle * (0.5 / math.pi))
    rest = angle - turns * 6.28125
    rest = rest - turns * (2.0 * math.pi - 6.28125)
    square = rest * rest
    cosine = jnp.full_like(square, COS_FIT[-1])
    for c in COS_FIT[-2::-1]:
        cosine = cosine * square + c
    sine = jnp.full_like(square, SIN_FIT[-1])
    for c in SIN_FIT[-2::-1]:
        sine = sine * square + c
    return cosine, sine * rest


def times(a, b):
    return a[0] * b[0] - a[1] * b[1], a[0] * b[1] + a[1] * b[0]


def total_of(values):
    total = values[0]
    for value in values[1:]:
        total = total + value
    return total


def rows_of(shape):
    return lax.broadcasted_iota(jnp.int32, shape, 0)


def between(rows, first, count):
    return ((rows - first) & 7) < count


def sum_rows(tiles):
    rows = rows_of((8, LANES))
    by_four = []
    for k, first in ((3, 0), (1, 6), (2, 7), (0, 5)):
        mask = between(rows, first, 4)
        here, there = tiles[k], tiles[k + 4]
        by_four.append(
            jnp.where(mask, here, there) + pltpu.roll(jnp.where(mask, there, here), 4, 0)
        )
    by_two = []
    for k, first in ((0, 2), (2, 1)):
        mask = between(rows, first, 2) | between(rows, first + 4, 2)
        here, there = by_four[k], by_four[k + 1]
        by_two.append(
            jnp.where(mask, here, there) + pltpu.roll(jnp.where(mask, there, here), 2, 0)
        )
    mask = (rows & 1) == 1
    here, there = by_two
    return jnp.where(mask, here, there) + pltpu.roll(jnp.where(mask, there, here), 1, 0)


def amplitude_kernel(
    pol_hbm, occ_hbm, dirs_hbm, orients_hbm, out, pol, occ, dirs, orients, sems, polf, lhs, rows, base, jump, table
):
    copies = [
        pltpu.make_async_copy(source, target, sems.at[k])
        for k, (source, target) in enumerate(
            ((dirs_hbm, dirs), (orients_hbm, orients), (pol_hbm, pol), (occ_hbm, occ))
        )
    ]
    for copy in copies:
        copy.start()
    orient_rank = lax.axis_index("orient")
    slab_rank = lax.axis_index("slab")
    plane = slab_rank.astype(jnp.float32)

    copies[0].wait()
    polar = (dirs[pl.ds(0, TILES, stride=2), :].astype(jnp.float32) + 0.5) * (math.pi / THETA_GRID)
    azimuth = dirs[pl.ds(1, TILES, stride=2), :].astype(jnp.float32) * (2.0 * math.pi / THETA_GRID)
    cos_polar, sin_polar = cos_sin(polar)
    cos_azimuth, sin_azimuth = cos_sin(azimuth)

    x1 = cos_sin(-wave_step * (sin_polar * cos_azimuth))
    y1 = cos_sin(-wave_step * (sin_polar * sin_azimuth))
    z = cos_sin(-wave_step * plane * cos_polar)
    x2 = times(x1, x1)
    x3 = times(x2, x1)
    x4 = times(x2, x2)
    x8 = times(x4, x4)
    fine = [None, x1, x2, x3, x4, times(x4, x1), times(x4, x2), times(x4, x3)]
    for k in range(8):
        value = times(z, fine[k]) if k else z
        for part in range(2):
            base[part, pl.ds(k, TILES, stride=8), :] = value[part]
    coarse = x4
    for k in range(6):
        rows[2 * k], rows[2 * k + 1] = coarse
        coarse = times(coarse, x8)
    rows[12], rows[13] = y1

    half = lax.broadcasted_iota(jnp.int32, (8, LANES), 1) < LANES // 2

    def make_table(tile, slot):
        start_re, start_im = base[0, 8 * tile : 8 * tile + 8, :], base[1, 8 * tile : 8 * tile + 8, :]
        y_re, y_im = rows[12, tile : tile + 1, :], rows[13, tile : tile + 1, :]
        strips = [None] * 12
        for k in range(6):
            turn_re, turn_im = rows[2 * k, tile : tile + 1, :], rows[2 * k + 1, tile : tile + 1, :]
            rr, ii, ri, ir = start_re * turn_re, start_im * turn_im, start_re * turn_im, start_im * turn_re
            strips[6 + k] = (rr - ii, ri + ir)
            strips[5 - k] = (rr + ii, ir - ri)
        twice = y_re + y_re
        for a in range(0, 12, 2):
            line = [[None, None] for _ in range(ROWS)]
            for k in range(2):
                v_re, v_im = strips[a + k]
                rr, ii, ri, ir = v_re * y_re, v_im * y_im, v_re * y_im, v_im * y_re
                after = (rr - ii, ri + ir)
                line[0][k] = (rr + ii, ir - ri)
                line[1][k] = (v_re, v_im)
                line[2][k] = after
                line[3][k] = (twice * after[0] - v_re, twice * after[1] - v_im)
            for y in range(ROWS):
                at = y * GX + 8 * a
                for part in range(2):
                    value = jnp.concatenate([line[y][0][part], line[y][1][part]], axis=0)
                    columns = slice(part * LANES, (part + 1) * LANES)
                    table[slot, at : at + 16, columns] = value.astype(jnp.bfloat16)

    def finish(tile, slot):
        product = jnp.dot(lhs[...], table[slot], preferred_element_type=jnp.float32)
        jump_re = jump[0, STEPS * tile : STEPS * tile + STEPS, :].reshape(3, 8, LANES)
        jump_im = jump[1, STEPS * tile : STEPS * tile + STEPS, :].reshape(3, 8, LANES)
        sums = []
        for group in range(12):
            at = STEPS * group
            c = [product[at + 8 * h : at + 8 * h + 8, :LANES] for h in range(3)]
            s = [product[at + 8 * h : at + 8 * h + 8, LANES:] for h in range(3)]
            real = total_of([c[h] * jump_re[h] for h in range(3)]) - total_of([s[h] * jump_im[h] for h in range(3)])
            imag = total_of([c[h] * jump_im[h] + s[h] * jump_re[h] for h in range(3)])
            sums.append((real, imag))
        row = [rows[14 + k, tile : tile + 1, :] for k in range(10)]
        result = []
        for part in range(2):
            tiles = []
            for incident in range(2):
                for o in range(2):
                    along = [sums[4 * c + 2 * incident + o][part] for c in range(3)]
                    tiles.append(total_of([along[c] * row[5 * o + c] for c in range(3)]))
            for incident in (1, 0):
                for o in range(2):
                    along = [sums[4 * c + 2 * incident + o][part] for c in range(2)]
                    tiles.append(total_of([along[c] * row[5 * o + 3 + c] for c in range(2)]))
            result.append(sum_rows(tiles))
        real, imag = result
        out[(2 * tile - FIRST_SLAB) % SLABS] = jnp.where(half, real, pltpu.roll(imag, LANES // 2, 1))
        out[(2 * tile + 1 - FIRST_SLAB) % SLABS] = jnp.where(half, pltpu.roll(real, LANES // 2, 1), imag)

    y2 = times(y1, y1)
    powers = [(jnp.ones_like(polar), jnp.zeros_like(polar)), times(y2, y2)]
    for k in range(2, STEPS):
        powers.append(times(powers[k // 2], powers[k - k // 2]))
    for k in range(STEPS):
        for part in range(2):
            jump[part, pl.ds(k, TILES, stride=STEPS), :] = powers[k][part]
    make_table(0, 0)

    for copy in copies[2:]:
        copy.wait()
    polf[...] = pol[...].astype(jnp.float32)
    for part in range(PARTS):
        mask = occ[pl.ds(part, STEPS, stride=PARTS), :].astype(jnp.float32)
        loaded = [
            polf[pl.ds(2 * part + incident, 6 * STEPS, stride=2 * PARTS), :].reshape(2, 3, STEPS, LANES)
            for incident in range(2)
        ]
        lhs[:, part * LANES : (part + 1) * LANES] = jnp.concatenate(
            [
                loaded[incident][o, c] * mask
                for c in range(3)
                for incident in range(2)
                for o in range(2)
            ],
            axis=0,
        ).astype(jnp.bfloat16)

    copies[1].wait()
    lane16 = lax.broadcasted_iota(jnp.int32, (1, ORIENTS), 1)
    turns = orients[0:1, :].astype(jnp.float32) * (2.0 * math.pi / ORIENT_GRID)
    weights = cos_sin((orients[1:2, :].astype(jnp.float32) + 0.5) * (math.pi / ORIENT_GRID))[1]
    shares = weights / (jnp.sum(weights, axis=1, keepdims=True) * float(GZ * GXY))
    for o in range(2):
        mine = lane16 == 2 * orient_rank + o
        turn = jnp.sum(jnp.where(mine, turns, 0.0), axis=1, keepdims=True)
        root = jnp.sqrt(jnp.sum(jnp.where(mine, shares, 0.0), axis=1, keepdims=True))
        cos_turn, sin_turn = cos_sin(azimuth - turn)
        cos_turn, sin_turn = cos_turn * root, sin_turn * root
        at = 14 + 5 * o
        rows[at] = cos_polar * cos_turn
        rows[at + 1] = cos_polar * sin_turn
        rows[at + 2] = -sin_polar * root
        rows[at + 3] = -sin_turn
        rows[at + 4] = cos_turn

    for tile in range(TILES):
        if tile + 1 < TILES:
            make_table(tile + 1, (tile + 1) % 2)
        finish(tile, tile % 2)


def mueller_kernel(parts, out):
    total = parts[0]
    for k in range(1, GZ):
        total = total + parts[k]
    other = pltpu.roll(total, 4, 0)
    lane = lax.broadcasted_iota(jnp.int32, (8, LANES), 1)
    side = jnp.where(rows_of((8, LANES)) < 4, 0.5, -0.5)
    turned = pltpu.roll(other, LANES // 2, 1) * jnp.where(lane < LANES // 2, -side, side)
    square = total * total
    elements = [0.5 * square, side * square, 0.5 * (total * other), total * turned]
    final = sum_rows(elements + elements)
    for k in range(out.shape[0]):
        out[k] = final


def average_kernel(parts, out):
    total = parts[0]
    for k in range(1, parts.shape[0]):
        total = total + parts[k]
    total = total + pltpu.roll(total, LANES // 2, 1)
    out[...] = total[0:4, : LANES // 2]


VMEM = pl.BlockSpec(memory_space=pltpu.VMEM)
HBM = pl.BlockSpec(memory_space=pltpu.HBM)


def exchange(blocks, axis, first):
    size = lax.axis_size(axis)
    group = [(first + k) % size for k in range(size)]
    return lax.all_to_all(blocks, axis, 0, 0, tiled=True, axis_index_groups=[group])


def amplitudes(polarization, occupied, orient_table, dir_index):
    pol = polarization.transpose(0, 2, 3, 1, 4).reshape(6, 2, GXY // LANES, LANES)
    pol = pol.transpose(0, 2, 1, 3).reshape(12 * GXY // LANES, LANES)
    occ = occupied.reshape(GXY // LANES, LANES)
    dirs = dir_index.T.reshape(2, TILES, LANES).transpose(1, 0, 2).reshape(2 * TILES, LANES)
    operands = (pol, occ, dirs, orient_table.T)
    return pl.pallas_call(
        amplitude_kernel,
        out_shape=pltpu.VMEM((GZ, 8, LANES), jnp.float32),
        in_specs=[HBM] * 4,
        out_specs=VMEM,
        scratch_shapes=[pltpu.VMEM(x.shape, x.dtype) for x in operands]
        + [
            pltpu.SemaphoreType.DMA((4,)),
            pltpu.VMEM(pol.shape, jnp.float32),
            pltpu.VMEM((12 * STEPS, CHUNK), jnp.bfloat16),
            pltpu.VMEM((24, TILES, LANES), jnp.float32),
            pltpu.VMEM((2, 8 * TILES, LANES), jnp.float32),
            pltpu.VMEM((2, STEPS * TILES, LANES), jnp.float32),
            pltpu.VMEM((2, CHUNK, 2 * LANES), jnp.bfloat16),
        ],
        compiler_params=pltpu.CompilerParams(vmem_limit_bytes=24 << 20),
        name="amplitude",
    )(*(pltpu.with_memory_space_constraint(x, pltpu.HBM) for x in operands))


def shards(polarization, occupied, orient_table, dir_index):
    amplitude = amplitudes(polarization, occupied, orient_table, dir_index)
    parts = exchange(amplitude, "slab", FIRST_SLAB)
    copies = pl.pallas_call(
        mueller_kernel,
        out_shape=pltpu.VMEM((lax.axis_size("orient"), 8, LANES), jnp.float32),
        in_specs=[VMEM],
        out_specs=VMEM,
        name="mueller",
    )(pltpu.with_memory_space_constraint(parts, pltpu.VMEM))
    parts = exchange(copies, "orient", FIRST_ORIENT)
    return pl.pallas_call(
        average_kernel,
        out_shape=jax.ShapeDtypeStruct((4, LANES // 2), jnp.float32),
        in_specs=[VMEM],
        out_specs=VMEM,
        name="average",
    )(pltpu.with_memory_space_constraint(parts, pltpu.VMEM))


def solution(mesh):
    return jax.shard_map(
        shards,
        mesh=mesh,
        in_specs=(P("orient", None, None, "slab", None), P("slab", None), P(), P()),
        out_specs=P(None, "slab"),
        check_vma=False,
    )
```
